128 devices in a mesh: dp: 32 (over y, x, z_hi), mp: 4 (over z_lo, core).
Axes of the slice: x: 4, y: 4, z: 4 (z_hi: 2, z_lo: 2; z = z_hi * 2 + z_lo), core: 2. Of those that a mesh axis runs over, the one named last changes fastest.
Arguments:
- image_in: bfloat16 [8192, 1408], P('dp'), may hold values from -8 to 8
- text_in: bfloat16 [8192, 1408], P('dp'), may hold values from -8 to 8
- image_gain: float32 [1408], replicated, may hold values from 0.25 to 1.75
- image_up: bfloat16 [1408, 6144], P(None, 'mp'), may hold values from -0.15625 to 0.15625
- image_down: bfloat16 [6144, 1408], P('mp'), may hold values from -0.078125 to 0.078125
- image_final: float32 [1408], replicated, may hold values from 0.25 to 1.75
- text_gain: float32 [1408], replicated, may hold values from 0.25 to 1.75
- text_up: bfloat16 [1408, 6144], P(None, 'mp'), may hold values from -0.15625 to 0.15625
- text_down: bfloat16 [6144, 1408], P('mp'), may hold values from -0.078125 to 0.078125
- text_final: float32 [1408], replicated, may hold values from 0.25 to 1.75
Outputs:
- image_grad: float32 [8192, 1408], P('dp')
- text_grad: float32 [8192, 1408], P('dp')
- row_loss: float32 [8192], P('dp')
The draws below stay inside these ranges and needn't reach their ends.
All inputs are finite; a program needn't handle non-finite values.
Results may differ from the reference program's by a relative error of at most 0.015.
Values may be sent and summed in bfloat16 or wider, within the bound.
No kernel may reach another device: no remote copies, remote signals or barrier semaphores. Data moves between devices by JAX's collectives and lax.ppermute only.
A program may use at most 128 MiB of HBM per device.

```python
import math
import jax
import jax.numpy as jnp
from jax import lax

D = 1408
FF = 6144
TOK_DEV = 256
TOKENS = 8192
N_DP = 32


def shared_signal(key):
    loadings = jax.random.normal(jax.random.fold_in(key, 101), (TOKENS, 8), jnp.float32)
    directions = jax.random.normal(jax.random.fold_in(key, 202), (8, D), jnp.float32)
    signal = loadings[:, 0:1] * directions[0:1, :]
    for latent_index in range(1, 8):
        signal = signal + loadings[:, latent_index:latent_index + 1] * directions[latent_index:latent_index + 1, :]
    return signal * (1.0 / math.sqrt(8.0))


def mixed_rows(signal, key):
    noise = jax.random.normal(key, (TOKENS, D), jnp.float32)
    mixed = 0.9219544 * signal + 0.3872983 * noise
    return jnp.clip(mixed, -8.0, 8.0).astype(jnp.bfloat16)


def draw_image_in(key, part):
    signal = shared_signal(key)
    key = jax.random.fold_in(key, 3)
    return mixed_rows(signal, key)


def draw_text_in(key, part):
    signal = shared_signal(key)
    key = jax.random.fold_in(key, 4)
    return mixed_rows(signal, key)


def block_levels(rng, dims, shards, least, top_value):
    level, own = 1.0, jax.random.fold_in(rng, 6)
    for position, shards_of in shards:
        heights = jnp.exp(jax.random.uniform(jax.random.fold_in(own, position), (shards_of,), jnp.float32, least / len(shards), top_value / len(shards)))
        level = level * jnp.repeat(heights, dims[position] // shards_of).reshape([-1 if axis == position else 1 for axis in range(len(dims))])
    return level


def scatter_about(stream_key, dims, spread, most, split=(), kind=jnp.bfloat16):
    drawn = spread * jax.random.normal(stream_key, dims, jnp.float32)
    if split:
        drawn = drawn * block_levels(stream_key, dims, split, -0.22, 0.18)
    return jnp.clip(drawn, -most, most).astype(kind)


def setup_inputs(seed: int = 0) -> dict:
    seeds = jax.random.split(jax.random.key(seed), 11)
    return {
        "image_in": draw_image_in(jax.random.fold_in(seeds[10], 71), 0),
        "text_in": draw_text_in(jax.random.fold_in(seeds[10], 71), 0),
        "image_gain": jnp.clip(1.0 + 0.15 * jax.random.normal(seeds[2], (D,), jnp.float32), 0.25, 1.75),
        "image_up": scatter_about(seeds[3], (D, FF), D ** -0.5, 0.15625, ((1, 4),)),
        "image_down": scatter_about(seeds[4], (FF, D), FF ** -0.5, 0.078125, ((0, 4),)),
        "image_final": jnp.clip(1.0 + 0.15 * jax.random.normal(seeds[5], (D,), jnp.float32), 0.25, 1.75),
        "text_gain": jnp.clip(1.0 + 0.15 * jax.random.normal(seeds[6], (D,), jnp.float32), 0.25, 1.75),
        "text_up": scatter_about(seeds[7], (D, FF), D ** -0.5, 0.15625, ((1, 4),)),
        "text_down": scatter_about(seeds[8], (FF, D), FF ** -0.5, 0.078125, ((0, 4),)),
        "text_final": jnp.clip(1.0 + 0.15 * jax.random.normal(seeds[9], (D,), jnp.float32), 0.25, 1.75),
    }


epsilon = 1e-06
logit_scale = 10.0
logit_bias = -1.0
loss_scale = 32768.0

def layer_norm(values, gain):
    center = lax.optimization_barrier(jnp.mean(values, axis=-1, keepdims=True))
    shifted = values - center
    variance = lax.optimization_barrier(jnp.mean(shifted * shifted, axis=-1, keepdims=True))
    return shifted * lax.rsqrt(variance + epsilon) * gain

def embed_rows(values, gain):
    normed = layer_norm(values, gain)
    return normed * lax.rsqrt(lax.optimization_barrier(jnp.sum(normed * normed, axis=-1, keepdims=True)) + epsilon)

def gelu_tanh(values):
    return jax.nn.gelu(values, approximate=True)

def tower_forward(tokens_in, gain, up_weight, down_weight):
    widened = tokens_in.astype(jnp.float32)
    normed = layer_norm(widened, gain).astype(jnp.bfloat16)
    pre_act = jnp.dot(normed, up_weight, preferred_element_type=jnp.float32)
    act_out = gelu_tanh(pre_act).astype(jnp.bfloat16)
    resid = widened + jnp.dot(act_out, down_weight, preferred_element_type=jnp.float32)
    return (widened, pre_act, resid)

def tower_backward(widened, gain, up_weight, down_weight, pre_act, resid, final_gain, d_embed):
    _, head_pull = jax.vjp(lambda values: embed_rows(values, final_gain), resid)
    d_resid = head_pull(d_embed)[0]
    d_act = lax.dot_general(d_resid.astype(jnp.bfloat16), down_weight, (((1,), (1,)), ((), ())), preferred_element_type=jnp.float32)
    _, act_pull = jax.vjp(gelu_tanh, pre_act)
    d_pre = act_pull(d_act)[0].astype(jnp.bfloat16)
    d_norm = lax.dot_general(d_pre, up_weight, (((1,), (1,)), ((), ())), preferred_element_type=jnp.float32)
    _, norm_pull = jax.vjp(lambda values: layer_norm(values, gain), widened)
    return d_resid + norm_pull(d_norm)[0]

def reference(image_in, text_in, image_gain, image_up, image_down, image_final, text_gain, text_up, text_down, text_final):
    image_wide, image_pre, image_resid = tower_forward(image_in, image_gain, image_up, image_down)
    text_wide, text_pre, text_resid = tower_forward(text_in, text_gain, text_up, text_down)
    z_image = embed_rows(image_resid, image_final).astype(jnp.bfloat16)
    z_text = embed_rows(text_resid, text_final).astype(jnp.bfloat16)
    text_ids = jnp.arange(TOKENS, dtype=jnp.int32)

    def pair_block(text_acc, index):
        start = index * TOK_DEV
        image_rows = lax.dynamic_slice_in_dim(z_image, start, TOK_DEV, 0)
        logits = logit_scale * lax.dot_general(image_rows, z_text, (((1,), (1,)), ((), ())), preferred_element_type=jnp.float32) + logit_bias
        image_ids = start + jnp.arange(TOK_DEV, dtype=jnp.int32)
        matched = image_ids[:, None] == text_ids[None, :]
        signed = jnp.where(matched, logits, -logits)
        row_terms = -lax.optimization_barrier(jnp.sum(jax.nn.log_sigmoid(signed), axis=1)) / TOKENS
        pair_grad = (loss_scale / TOKENS * (jax.nn.sigmoid(logits) - matched.astype(jnp.float32))).astype(jnp.bfloat16)
        to_image = jnp.dot(pair_grad, z_text, preferred_element_type=jnp.float32)
        to_text = lax.dot_general(pair_grad, image_rows, (((0,), (0,)), ((), ())), preferred_element_type=jnp.float32)
        return (text_acc + to_text, (row_terms, to_image))
    text_zero = jnp.zeros((TOKENS, D), jnp.float32)
    text_acc, (row_terms, to_image) = lax.scan(pair_block, text_zero, jnp.arange(N_DP, dtype=jnp.int32))
    row_loss = row_terms.reshape(TOKENS)
    d_image = logit_scale * to_image.reshape(TOKENS, D)
    d_text = logit_scale * text_acc
    image_grad = tower_backward(image_wide, image_gain, image_up, image_down, image_pre, image_resid, image_final, d_image)
    text_grad = tower_backward(text_wide, text_gain, text_up, text_down, text_pre, text_resid, text_final, d_text)
    return (image_grad, text_grad, row_loss)
```

```python
import jax
import jax.numpy as jnp
import numpy as np
from jax import lax
from jax.sharding import PartitionSpec as P

epsilon = 1e-06
logit_scale = 10.0
logit_bias = -1.0
loss_scale = 32768.0
total_rows = 8192

AXES = ("dp", "mp")
DIMS = (4, 4, 2, 2, 2)
bf16 = jnp.bfloat16
f32 = jnp.float32


def routes(move):
    pairs = []
    for source in range(128):
        y, x, z_hi, z_lo, core = (int(v) for v in np.unravel_index(source, DIMS))
        y, x, z, core = move(y, x, 2 * z_hi + z_lo, core)
        y, x, z = y % 4, x % 4, z % 4
        target = np.ravel_multi_index((y, x, z // 2, z % 2, core), DIMS)
        pairs.append((source, int(target)))
    return pairs


def first_ring(steps):
    return routes(lambda y, x, z, c: (y, x + steps, z, c) if c == 0 else (y + steps, x, z, c))


def second_ring(steps):
    return routes(lambda y, x, z, c: (y + steps, x, z, c) if c == 0 else (y, x + steps, z, c))


def z_ring(steps):
    return routes(lambda y, x, z, c: (y, x, z + steps, c))


SIBLING = routes(lambda y, x, z, c: (y, x, z, 1 - c))
Z_PAIR = routes(lambda y, x, z, c: (y, x, z ^ 1, c))
Z_OUT = routes(lambda y, x, z, c: (y, x, z + 1 - 2 * c, c))
Z_BACK = routes(lambda y, x, z, c: (y, x, z - 1 + 2 * c, c))


def send(value, pairs):
    return lax.ppermute(value, AXES, pairs)


def layer_norm(values, gain):
    center = jnp.mean(values, axis=-1, keepdims=True)
    shifted = values - center
    variance = jnp.mean(shifted * shifted, axis=-1, keepdims=True)
    return shifted * lax.rsqrt(variance + epsilon) * gain


def embed_rows(values, gain):
    normed = layer_norm(values, gain)
    return normed * lax.rsqrt(jnp.sum(normed * normed, axis=-1, keepdims=True) + epsilon)


def gelu_tanh(values):
    return jax.nn.gelu(values, approximate=True)


def contract(a, b, dims):
    return lax.dot_general(a, b, (dims, ((), ())), preferred_element_type=f32)


def tower_forward(tokens, gain, up, down):
    normed = layer_norm(tokens.astype(f32), gain).astype(bf16)
    pre_act = contract(normed, up, ((1,), (0,)))
    act_out = gelu_tanh(pre_act).astype(bf16)
    return pre_act, contract(act_out, down, ((1,), (0,)))


def scatter_rows(partial):
    half = partial[:128] + send(partial[128:].astype(bf16), SIBLING).astype(f32)
    return half[:64] + send(half[64:].astype(bf16), Z_PAIR).astype(f32)


def gather_rows(own):
    half = jnp.concatenate([own, send(own, Z_PAIR)], 0)
    return jnp.concatenate([half, send(half, SIBLING)], 0)


def gather_plane(own):
    before = send(own, first_ring(1))
    after = send(own, first_ring(-1))
    across = send(own, first_ring(2))
    near = jnp.concatenate([own, before, across, after], 0)
    left = send(near, second_ring(1))
    right = send(near, second_ring(-1))
    far = jnp.concatenate(
        [send(left[:128], second_ring(1)), send(right[128:], second_ring(-1))], 0
    )
    return near, left, right, far


def scatter_plane(near, left, right, far):
    far = far.astype(bf16)
    left = jnp.concatenate(
        [left[:128] + send(far[:128], second_ring(-1)).astype(f32), left[128:]], 0
    )
    right = jnp.concatenate(
        [right[:128], right[128:] + send(far[128:], second_ring(1)).astype(f32)], 0
    )
    near = (
        near
        + send(left.astype(bf16), second_ring(-1)).astype(f32)
        + send(right.astype(bf16), second_ring(1)).astype(f32)
    )
    rest = near[64:].astype(bf16)
    return (
        near[:64]
        + send(rest[:64], first_ring(-1)).astype(f32)
        + send(rest[64:128], first_ring(2)).astype(f32)
        + send(rest[128:], first_ring(1)).astype(f32)
    )


def gather_column(own, core):
    below = send(own, z_ring(1))
    above = send(own, z_ring(-1))
    across = send(jnp.where(core == 0, below, above), Z_OUT)
    near = jnp.concatenate([own, below, above], 0)
    return jnp.concatenate([near, across, send(near, SIBLING), send(across, SIBLING)], 0)


def packed(values, loss):
    high = loss.astype(bf16)
    low = (loss - high.astype(f32)).astype(bf16)
    pad = jnp.zeros((loss.shape[0], 126), bf16)
    return jnp.concatenate([values.astype(bf16), high, low, pad], 1)


def unpacked(both):
    wide = both.astype(f32)
    return wide[:, :1408], wide[:, 1408:1409] + wide[:, 1409:1410]


def plus(pair, both):
    values, loss = unpacked(both)
    return pair[0] + values, pair[1] + loss


def rows_of(pair, start, count):
    return pair[0][start : start + count], pair[1][start : start + count]


def scatter_column(values, loss, core):
    pair = plus((values[:256], loss[:256]), send(packed(values[256:], loss[256:]), SIBLING))
    across = send(packed(*rows_of(pair, 192, 64)), Z_BACK)
    none = jnp.zeros_like(across)
    below = plus(rows_of(pair, 64, 64), jnp.where(core == 0, across, none))
    above = plus(rows_of(pair, 128, 64), jnp.where(core == 1, across, none))
    own = plus(rows_of(pair, 0, 64), send(packed(*below), z_ring(-1)))
    return plus(own, send(packed(*above), z_ring(1)))


def pair_tile(images, texts, has_own):
    logits = logit_scale * contract(images, texts, ((1,), (1,))) + logit_bias
    grown = jnp.exp(logits)
    softplus = jnp.log1p(grown)
    share = grown / (1.0 + grown)
    if has_own:
        row = lax.broadcasted_iota(jnp.int32, logits.shape, 0)
        column = lax.broadcasted_iota(jnp.int32, logits.shape, 1)
        matched = (row == column) & (row < 64)
        softplus = jnp.where(matched, softplus - logits, softplus)
        share = jnp.where(matched, share - 1.0, share)
    loss = jnp.sum(softplus, axis=1, keepdims=True) / total_rows
    pair_grad = (loss_scale / total_rows * share).astype(bf16)
    to_image = contract(pair_grad, texts, ((1,), (0,)))
    to_text = contract(pair_grad, images, ((0,), (0,)))
    return loss, to_image, to_text


def head_back(resid, gain, d_embed):
    _, pull = jax.vjp(lambda values: embed_rows(values, gain), resid)
    return pull(d_embed)[0]


def tower_backward(d_resid, up, down, pre_act):
    d_act = contract(d_resid, down, ((1,), (1,)))
    _, pull = jax.vjp(gelu_tanh, pre_act)
    d_pre = pull(d_act)[0].astype(bf16)
    return contract(d_pre, up, ((1,), (1,)))


def input_grad(tokens, gain, d_resid, d_norm_part, z_lo):
    half = d_norm_part[:128] + send(d_norm_part[128:].astype(bf16), SIBLING).astype(f32)
    half = half.astype(bf16)
    other = send(half, Z_PAIR)
    other = jnp.concatenate([other[64:], other[:64]], 0)
    d_norm = half.astype(f32) + other.astype(f32)
    _, pull = jax.vjp(lambda values: layer_norm(values, gain), tokens[:128].astype(f32))
    grad = d_resid[:128].astype(f32) + pull(d_norm)[0]
    return jnp.where(z_lo == 0, grad, jnp.concatenate([grad[64:], grad[:64]], 0))


def whole_rows(grad, core):
    other = send(grad, SIBLING)
    return jnp.where(
        core == 0, jnp.concatenate([grad, other], 0), jnp.concatenate([other, grad], 0)
    )


def on_device(
    image_in,
    text_in,
    image_gain,
    image_up,
    image_down,
    image_final,
    text_gain,
    text_up,
    text_down,
    text_final,
):
    mp = lax.axis_index("mp")
    z_lo, core = mp // 2, mp % 2
    mine = 2 * core + z_lo

    def relative(rows):
        blocks = [
            lax.dynamic_slice_in_dim(rows, (place ^ mine) * 64, 64, 0) for place in range(4)
        ]
        return jnp.concatenate(blocks, 0)

    texts = relative(text_in)
    images = relative(image_in)
    text_pre, text_part = tower_forward(texts, text_gain, text_up, text_down)
    text_resid = texts[:64].astype(f32) + scatter_rows(text_part)
    z_text = embed_rows(text_resid, text_final).astype(bf16)
    text_blocks = gather_plane(z_text)
    image_pre, image_part = tower_forward(images, image_gain, image_up, image_down)
    image_resid = images[:64].astype(f32) + scatter_rows(image_part)
    z_image = embed_rows(image_resid, image_final).astype(bf16)
    image_block = gather_column(z_image, core)

    terms = [pair_tile(image_block, block, i == 0) for i, block in enumerate(text_blocks)]
    to_image = logit_scale * sum(term[1] for term in terms)
    loss = sum(term[0] for term in terms)
    d_text = scatter_plane(*[logit_scale * term[2] for term in terms])
    d_image, loss = scatter_column(to_image, loss, core)

    image_dres, losses = unpacked(
        gather_rows(packed(head_back(image_resid, image_final, d_image), loss))
    )
    image_dres = image_dres.astype(bf16)
    image_dnorm = tower_backward(image_dres, image_up, image_down, image_pre)
    image_half = input_grad(images, image_gain, image_dres, image_dnorm, z_lo)
    image_grad = whole_rows(image_half, core)

    text_dres = gather_rows(head_back(text_resid, text_final, d_text).astype(bf16))
    text_dnorm = tower_backward(text_dres, text_up, text_down, text_pre)
    text_half = input_grad(texts, text_gain, text_dres, text_dnorm, z_lo)
    text_grad = whole_rows(text_half, core)
    return (image_grad, text_grad, relative(losses).reshape(256))


def solution(mesh):
    placed = (
        P("dp", None),
        P("dp", None),
        P(),
        P(None, "mp"),
        P("mp", None),
        P(),
        P(),
        P(None, "mp"),
        P("mp", None),
        P(),
    )
    return jax.shard_map(
        on_device,
        mesh=mesh,
        in_specs=placed,
        out_specs=(P("dp", None), P("dp", None), P("dp")),
        check_vma=False,
    )
```

```python
import functools

import jax
import jax.numpy as jnp
import numpy as np
from jax import lax
from jax.experimental import pallas as pl
from jax.experimental.pallas import tpu as pltpu
from jax.sharding import PartitionSpec as P

epsilon = 1e-06
logit_scale = 10.0
logit_bias = -1.0
loss_scale = 32768.0
total_rows = 8192.0

WIDTH = 1408
HIDDEN = 1536
PACKED = 1536
BLOCK = 64
FF_STEP = 256
AXES = ("dp", "mp")
DIMS = (4, 4, 2, 2, 2)
bf16 = jnp.bfloat16
f32 = jnp.float32


def routes(move):
    pairs = []
    for source in range(128):
        y, x, z_hi, z_lo, core = (int(v) for v in np.unravel_index(source, DIMS))
        y, x, z, core = move(y, x, 2 * z_hi + z_lo, core)
        y, x, z = y % 4, x % 4, z % 4
        target = np.ravel_multi_index((y, x, z // 2, z % 2, core), DIMS)
        pairs.append((source, int(target)))
    return pairs


def first_ring(steps):
    return routes(lambda y, x, z, c: (y, x + steps, z, c) if c == 0 else (y + steps, x, z, c))


def second_ring(steps):
    return routes(lambda y, x, z, c: (y + steps, x, z, c) if c == 0 else (y, x + steps, z, c))


SIBLING = routes(lambda y, x, z, c: (y, x, z, 1 - c))
Z_PAIR = routes(lambda y, x, z, c: (y, x, z ^ 1, c))
Z_OUT = routes(lambda y, x, z, c: (y, x, z + 1 - 2 * c, c))
Z_BACK = routes(lambda y, x, z, c: (y, x, z - 1 + 2 * c, c))


def send(value, pairs):
    return lax.ppermute(value, AXES, pairs)


def contract(a, b, left, right):
    return lax.dot_general(a, b, (((left,), (right,)), ((), ())), preferred_element_type=f32)


def call(body, outs, args, scalar=None, flops=1 << 20, **options):
    specs = [pl.BlockSpec(memory_space=pltpu.VMEM) for _ in args]
    if scalar is not None:
        specs = [pl.BlockSpec(memory_space=pltpu.SMEM)] + specs
        args = [scalar] + list(args)
    moved = sum(int(np.prod(o.shape)) * o.dtype.itemsize for o in outs)
    moved += sum(int(np.prod(a.shape)) * a.dtype.itemsize for a in args)
    return pl.pallas_call(
        body,
        out_shape=outs,
        in_specs=specs,
        out_specs=[pl.BlockSpec(memory_space=pltpu.VMEM) for _ in outs],
        compiler_params=pltpu.CompilerParams(vmem_limit_bytes=30 << 20),
        cost_estimate=pl.CostEstimate(flops=flops, bytes_accessed=moved, transcendentals=0),
        **options,
    )(*args)


def shape(rows, columns, kind):
    return jax.ShapeDtypeStruct((rows, columns), kind)


def centred(values):
    center = jnp.mean(values, axis=-1, keepdims=True)
    shifted = values - center
    variance = jnp.mean(shifted * shifted, axis=-1, keepdims=True)
    inverse = lax.rsqrt(variance + epsilon)
    return shifted * inverse, inverse


def centred_back(unit, inverse, d_unit):
    along = jnp.mean(d_unit * unit, axis=-1, keepdims=True)
    return inverse * (d_unit - jnp.mean(d_unit, axis=-1, keepdims=True) - unit * along)


def pack(out_ref, start, values, loss):
    rows = values.shape[0]
    column = lax.broadcasted_iota(jnp.int32, (rows, 128), 1)
    high = loss.astype(bf16).astype(f32)
    tail = jnp.where(column == 0, high, jnp.where(column == 1, loss - high, 0.0))
    out_ref[pl.ds(start, rows), 0:WIDTH] = values.astype(out_ref.dtype)
    out_ref[pl.ds(start, rows), WIDTH:PACKED] = tail.astype(out_ref.dtype)


def loss_of(tail):
    return jnp.sum(tail.astype(f32), axis=-1, keepdims=True)


SLOPE = 0.7978845608028654
CUBIC = 0.044715


def forward_body(mine, x_ref, gain_ref, up_ref, down_ref, pre_ref, keep_ref, send_ref, norm, total):
    step = pl.program_id(0)

    @pl.when(step == 0)
    def _():
        for place in range(4):
            start = pl.multiple_of((place ^ mine[0]) * BLOCK, BLOCK)
            unit, _ = centred(x_ref[pl.ds(start, BLOCK), :].astype(f32))
            norm[place * BLOCK : (place + 1) * BLOCK, :] = (unit * gain_ref[...]).astype(bf16)

    pre = contract(norm[...], up_ref[...], 1, 0)
    pre_ref[...] = pre
    act = 0.5 * pre * (1.0 + jnp.tanh(SLOPE * (pre + CUBIC * pre * pre * pre)))
    part = contract(act.astype(bf16), down_ref[...], 1, 0)

    @pl.when(step == 0)
    def _():
        total[...] = part

    @pl.when(step > 0)
    def _():
        total[...] += part

    @pl.when(step == pl.num_programs(0) - 1)
    def _():
        keep_ref[...] = total[0:128, :]
        send_ref[...] = total[128:256, :].astype(bf16)


def tower_forward(mine, tokens, gain, up, down):
    steps = HIDDEN // FF_STEP
    fixed = lambda i, m: (0, 0)
    return pl.pallas_call(
        forward_body,
        grid_spec=pltpu.PrefetchScalarGridSpec(
            num_scalar_prefetch=1,
            grid=(steps,),
            in_specs=[
                pl.BlockSpec((256, WIDTH), fixed),
                pl.BlockSpec((1, WIDTH), fixed),
                pl.BlockSpec((WIDTH, FF_STEP), lambda i, m: (0, i)),
                pl.BlockSpec((FF_STEP, WIDTH), lambda i, m: (i, 0)),
            ],
            out_specs=[
                pl.BlockSpec((256, FF_STEP), lambda i, m: (0, i)),
                pl.BlockSpec((128, WIDTH), fixed),
                pl.BlockSpec((128, WIDTH), fixed),
            ],
            scratch_shapes=[pltpu.VMEM((256, WIDTH), bf16), pltpu.VMEM((256, WIDTH), f32)],
        ),
        out_shape=[shape(256, HIDDEN, f32), shape(128, WIDTH, f32), shape(128, WIDTH, bf16)],
        compiler_params=pltpu.CompilerParams(vmem_limit_bytes=30 << 20),
        cost_estimate=pl.CostEstimate(
            flops=4 * 256 * WIDTH * HIDDEN, bytes_accessed=12 << 20, transcendentals=256 * HIDDEN
        ),
    )(mine, tokens, gain.reshape(1, WIDTH), up, down)


def backward_body(r0, r1, r2, r3, pre_ref, up_ref, down_ref, keep_ref, send_ref, given, total):
    step = pl.program_id(0)

    @pl.when(step == 0)
    def _():
        for place, ref in enumerate((r0, r1, r2, r3)):
            given[place * BLOCK : (place + 1) * BLOCK, :] = ref[:, 0:WIDTH]

    d_act = contract(given[...], down_ref[...], 1, 1)
    pre = pre_ref[...]
    square = pre * pre
    curve = jnp.tanh(SLOPE * pre * (1.0 + CUBIC * square))
    slope = 0.5 * (1.0 + curve) + 0.5 * pre * (1.0 - curve * curve) * (
        SLOPE * (1.0 + 3.0 * CUBIC * square)
    )
    part = contract((d_act * slope).astype(bf16), up_ref[...], 1, 1)

    @pl.when(step == 0)
    def _():
        total[...] = part

    @pl.when(step > 0)
    def _():
        total[...] += part

    @pl.when(step == pl.num_programs(0) - 1)
    def _():
        keep_ref[...] = total[0:128, :]
        send_ref[...] = total[128:256, :].astype(bf16)


def tower_backward(blocks, pre, up, down):
    steps = HIDDEN // FF_STEP
    fixed = lambda i: (0, 0)
    return pl.pallas_call(
        backward_body,
        grid=(steps,),
        in_specs=[pl.BlockSpec(block.shape, fixed) for block in blocks]
        + [
            pl.BlockSpec((256, FF_STEP), lambda i: (0, i)),
            pl.BlockSpec((WIDTH, FF_STEP), lambda i: (0, i)),
            pl.BlockSpec((FF_STEP, WIDTH), lambda i: (i, 0)),
        ],
        out_specs=[pl.BlockSpec((128, WIDTH), fixed), pl.BlockSpec((128, WIDTH), fixed)],
        scratch_shapes=[pltpu.VMEM((256, WIDTH), bf16), pltpu.VMEM((256, WIDTH), f32)],
        out_shape=[shape(128, WIDTH, f32), shape(128, WIDTH, bf16)],
        compiler_params=pltpu.CompilerParams(vmem_limit_bytes=30 << 20),
        cost_estimate=pl.CostEstimate(
            flops=4 * 256 * WIDTH * HIDDEN, bytes_accessed=12 << 20, transcendentals=256 * HIDDEN
        ),
    )(*blocks, pre, up, down)


def halve_body(keep_ref, got_ref, own_ref, send_ref):
    own_ref[...] = keep_ref[0:BLOCK, :] + got_ref[0:BLOCK, :].astype(f32)
    send_ref[...] = (keep_ref[BLOCK:128, :] + got_ref[BLOCK:128, :].astype(f32)).astype(bf16)


def embed_body(mine, own_ref, got_ref, x_ref, gain_ref, resid_ref, z_ref):
    start = pl.multiple_of(mine[0] * BLOCK, BLOCK)
    resid = own_ref[...] + got_ref[...].astype(f32) + x_ref[pl.ds(start, BLOCK), :].astype(f32)
    resid_ref[...] = resid
    normed = centred(resid)[0] * gain_ref[...]
    scale = lax.rsqrt(jnp.sum(normed * normed, axis=-1, keepdims=True) + epsilon)
    z_ref[...] = (normed * scale).astype(bf16)


def scattered_embed(mine, keep, sent, tokens, final_gain):
    got = send(sent, SIBLING)
    own, sent = call(halve_body, [shape(BLOCK, WIDTH, f32), shape(BLOCK, WIDTH, bf16)], [keep, got])
    got = send(sent, Z_PAIR)
    return call(
        embed_body,
        [shape(BLOCK, WIDTH, f32), shape(BLOCK, WIDTH, bf16)],
        [own, got, tokens, final_gain.reshape(1, WIDTH)],
        scalar=mine,
    )


def stack_body(first_ref, second_ref, out_ref):
    out_ref[0:BLOCK, :] = first_ref[...]
    out_ref[BLOCK:128, :] = second_ref[...]


def stacked(first, second):
    return call(stack_body, [shape(128, WIDTH, bf16)], [first, second])[0]


def gather_plane(own):
    before = send(own, first_ring(1))
    across = send(own, first_ring(2))
    after = send(own, first_ring(-1))
    near = (stacked(own, before), stacked(after, across))
    left = [send(near[0], second_ring(1)), None]
    right = [None, send(near[1], second_ring(-1))]
    left[1] = send(near[1], second_ring(1))
    right[0] = send(near[0], second_ring(-1))
    far = (send(left[0], second_ring(1)), send(right[1], second_ring(-1)))
    return near, left, right, far


def gather_column(own):
    ahead = send(own, Z_OUT)
    behind = send(own, Z_BACK)
    across = send(ahead, Z_OUT)
    blocks = [own, ahead, behind, across]
    return blocks + [send(block, SIBLING) for block in blocks]


def pair_chunk(images, texts, has_own):
    logits = logit_scale * contract(images, texts, 1, 1) + logit_bias
    grown = jnp.exp(logits)
    softplus = jnp.log1p(grown)
    share = grown / (1.0 + grown)
    if has_own:
        row = lax.broadcasted_iota(jnp.int32, logits.shape, 0)
        column = lax.broadcasted_iota(jnp.int32, logits.shape, 1)
        matched = (row == column) & (row < BLOCK)
        softplus = jnp.where(matched, softplus - logits, softplus)
        share = jnp.where(matched, share - 1.0, share)
    loss = jnp.sum(softplus, axis=1, keepdims=True) / total_rows
    pair_grad = (loss_scale / total_rows * share).astype(bf16)
    to_image = logit_scale * contract(pair_grad, texts, 1, 0)
    to_text = logit_scale * contract(pair_grad, images, 0, 0)
    return loss, to_image, to_text


def early_body(*refs):
    image_refs, refs = refs[:8], refs[8:]
    near0, near1, left0, left1, right0, right1 = refs[:6]
    image_ref, total_ref, loss_ref, near_ref, left_keep, left_send, right_send, right_keep = refs[6:14]
    texts = refs[14]
    for place, ref in enumerate(image_refs):
        image_ref[place * BLOCK : (place + 1) * BLOCK, :] = ref[...]
    losses = 0.0
    for chunk, parts in enumerate(((near0, near1), (left0, left1), (right0, right1))):
        texts[0:128, :] = parts[0][...]
        texts[128:256, :] = parts[1][...]
        loss, to_image, to_text = pair_chunk(image_ref[...], texts[...], chunk == 0)
        losses = losses + loss
        if chunk == 0:
            total_ref[...] = to_image
            near_ref[...] = to_text
        else:
            total_ref[...] += to_image
            halves = (left_keep, left_send) if chunk == 1 else (right_send, right_keep)
            halves[0][...] = to_text[0:128, :].astype(halves[0].dtype)
            halves[1][...] = to_text[128:256, :].astype(halves[1].dtype)
    loss_ref[...] = jnp.broadcast_to(losses, (512, 128))


def late_body(image_ref, total_ref, loss_ref, far0, far1, far0_ref, far1_ref, keep_ref, send_ref, texts):
    texts[0:128, :] = far0[...]
    texts[128:256, :] = far1[...]
    loss, to_image, to_text = pair_chunk(image_ref[...], texts[...], False)
    far0_ref[...] = to_text[0:128, :].astype(bf16)
    far1_ref[...] = to_text[128:256, :].astype(bf16)
    loss = loss + loss_ref[:, 0:1]
    to_image = to_image + total_ref[...]
    pack(keep_ref, 0, to_image[0:256, :], loss[0:256, :])
    pack(send_ref, 0, to_image[256:512, :], loss[256:512, :])


def pair_tile(images, near, left, right, far):
    half32, half16 = shape(128, WIDTH, f32), shape(128, WIDTH, bf16)
    image, total, loss, near_grad, left_keep, left_send, right_send, right_keep = call(
        early_body,
        [shape(512, WIDTH, bf16), shape(512, WIDTH, f32), shape(512, 128, f32)]
        + [shape(256, WIDTH, f32), half32, half16, half16, half32],
        [*images, *near, *left, *right],
        flops=6 * 512 * 768 * WIDTH,
        scratch_shapes=[pltpu.VMEM((256, WIDTH), bf16)],
    )
    far0, far1, image_keep, image_send = call(
        late_body,
        [half16, half16, shape(256, PACKED, f32), shape(256, PACKED, bf16)],
        [image, total, loss, *far],
        flops=6 * 512 * 256 * WIDTH,
        scratch_shapes=[pltpu.VMEM((256, WIDTH), bf16)],
    )
    return near_grad, left_keep, left_send, right_send, right_keep, far0, far1, image_keep, image_send


def joined_body(keep_ref, got_ref, out_ref):
    out_ref[...] = (keep_ref[...] + got_ref[...].astype(f32)).astype(out_ref.dtype)


def near_body(near_ref, l0, l1, r0, r1, own_ref, before_ref, after_ref, across_ref):
    first = near_ref[0:128, :] + l0[...].astype(f32) + r0[...].astype(f32)
    second = near_ref[128:256, :] + l1[...].astype(f32) + r1[...].astype(f32)
    own_ref[...] = first[0:BLOCK, :]
    before_ref[...] = first[BLOCK:128, :].astype(bf16)
    after_ref[...] = second[0:BLOCK, :].astype(bf16)
    across_ref[...] = second[BLOCK:128, :].astype(bf16)


def head_back(resid, gain, d_embed):
    unit, inverse = centred(resid)
    normed = unit * gain
    scale = lax.rsqrt(jnp.sum(normed * normed, axis=-1, keepdims=True) + epsilon)
    along = jnp.sum(d_embed * normed, axis=-1, keepdims=True)
    d_normed = scale * d_embed - normed * (scale * scale * scale * along)
    return centred_back(unit, inverse, d_normed * gain)


def text_head_body(own_ref, before_ref, after_ref, across_ref, resid_ref, gain_ref, out_ref):
    d_embed = own_ref[...] + before_ref[...].astype(f32)
    d_embed = d_embed + after_ref[...].astype(f32) + across_ref[...].astype(f32)
    out_ref[...] = head_back(resid_ref[...], gain_ref[...], d_embed).astype(bf16)


def scatter_plane(grads, resid, gain):
    near, left_keep, left_send, right_send, right_keep, far0, far1 = grads
    half16, block16 = shape(128, WIDTH, bf16), shape(BLOCK, WIDTH, bf16)
    l1 = send(left_send, second_ring(-1))
    r0 = send(right_send, second_ring(1))
    got0 = send(far0, second_ring(-1))
    got1 = send(far1, second_ring(1))
    l0 = send(call(joined_body, [half16], [left_keep, got0])[0], second_ring(-1))
    r1 = send(call(joined_body, [half16], [right_keep, got1])[0], second_ring(1))
    own, before, after, across = call(
        near_body, [shape(BLOCK, WIDTH, f32), block16, block16, block16], [near, l0, l1, r0, r1]
    )
    across = send(across, first_ring(2))
    before = send(before, first_ring(-1))
    after = send(after, first_ring(1))
    return call(text_head_body, [block16], [own, before, after, across, resid, gain.reshape(1, WIDTH)])[0]


def add_packed(values, loss, ref, start):
    rows = values.shape[0]
    return (
        values + ref[start : start + rows, 0:WIDTH].astype(f32),
        loss + loss_of(ref[start : start + rows, WIDTH:PACKED]),
    )


def packed_rows(ref, start, rows):
    return ref[start : start + rows, 0:WIDTH], loss_of(ref[start : start + rows, WIDTH:PACKED])


def column_first_body(keep_ref, got_ref, near_ref, across_ref):
    for place in range(3):
        values, loss = packed_rows(keep_ref, place * BLOCK, BLOCK)
        pack(near_ref, place * BLOCK, *add_packed(values, loss, got_ref, place * BLOCK))
    values, loss = packed_rows(keep_ref, 3 * BLOCK, BLOCK)
    pack(across_ref, 0, *add_packed(values, loss, got_ref, 3 * BLOCK))


def column_second_body(near_ref, got_ref, ahead_ref, behind_ref):
    values, loss = packed_rows(near_ref, BLOCK, BLOCK)
    pack(ahead_ref, 0, *add_packed(values, loss, got_ref, 0))
    pack(behind_ref, 0, *packed_rows(near_ref, 2 * BLOCK, BLOCK))


def image_head_body(near_ref, ahead_ref, behind_ref, resid_ref, gain_ref, out_ref):
    values, loss = packed_rows(near_ref, 0, BLOCK)
    values, loss = add_packed(values, loss, ahead_ref, 0)
    values, loss = add_packed(values, loss, behind_ref, 0)
    pack(out_ref, 0, head_back(resid_ref[...], gain_ref[...], values), loss)


def scatter_column(keep, sent, resid, gain):
    block16 = shape(BLOCK, PACKED, bf16)
    got = send(sent, SIBLING)
    near, across = call(column_first_body, [shape(3 * BLOCK, PACKED, f32), block16], [keep, got])
    got = send(across, Z_BACK)
    ahead, behind = call(column_second_body, [block16, block16], [near, got])
    ahead = send(ahead, Z_BACK)
    behind = send(behind, Z_OUT)
    return call(image_head_body, [block16], [near, ahead, behind, resid, gain.reshape(1, WIDTH)])[0]


def gather_rows(own):
    other = send(own, Z_PAIR)
    return own, other, send(own, SIBLING), send(other, SIBLING)


def swapped_body(own_ref, got_ref, out_ref):
    own, got = own_ref[...].astype(f32), got_ref[...].astype(f32)
    out_ref[0:BLOCK, :] = (own[0:BLOCK, :] + got[BLOCK:128, :]).astype(bf16)
    out_ref[BLOCK:128, :] = (own[BLOCK:128, :] + got[0:BLOCK, :]).astype(bf16)


def grad_body(has_loss, mine, x_ref, gain_ref, r0, r1, r2, r3, own_ref, got_ref, out_ref, *loss_ref):
    losses = jnp.zeros((1, 256), f32)
    for place, ref in enumerate((r0, r1, r2, r3)):
        target = place ^ mine[0]
        start = pl.multiple_of(target * BLOCK, BLOCK)
        unit, inverse = centred(x_ref[pl.ds(start, BLOCK), :].astype(f32))
        half = own_ref if place < 2 else got_ref
        first = (place % 2) * BLOCK
        d_norm = half[first : first + BLOCK, :].astype(f32)
        back = centred_back(unit, inverse, d_norm * gain_ref[...])
        out_ref[pl.ds(start, BLOCK), :] = ref[:, 0:WIDTH].astype(f32) + back
        if has_loss:
            row = lax.broadcasted_iota(jnp.int32, (BLOCK, 256), 0)
            column = lax.broadcasted_iota(jnp.int32, (BLOCK, 256), 1)
            spread = jnp.where(column == target * BLOCK + row, loss_of(ref[:, WIDTH:PACKED]), 0.0)
            losses = losses + jnp.sum(spread, axis=0, keepdims=True)
    if has_loss:
        loss_ref[0][...] = losses


def input_grad(mine, tokens, gain, blocks, keep, sent, has_loss):
    half16 = shape(128, WIDTH, bf16)
    got = send(sent, SIBLING)
    half = call(joined_body, [half16], [keep, got])[0]
    got = send(half, Z_PAIR)
    own = call(swapped_body, [half16], [half, got])[0]
    got = send(own, SIBLING)
    outs = [shape(256, WIDTH, f32)] + ([shape(1, 256, f32)] if has_loss else [])
    return call(
        functools.partial(grad_body, has_loss),
        outs,
        [tokens, gain.reshape(1, WIDTH), *blocks, own, got],
        scalar=mine,
    )


def on_device(
    image_in,
    text_in,
    image_gain,
    image_up,
    image_down,
    image_final,
    text_gain,
    text_up,
    text_down,
    text_final,
):
    mp = lax.axis_index("mp")
    mine = (2 * (mp % 2) + mp // 2).astype(jnp.int32).reshape(1)

    text_pre, keep, sent = tower_forward(mine, text_in, text_gain, text_up, text_down)
    text_resid, z_text = scattered_embed(mine, keep, sent, text_in, text_final)
    near, left, right, far = gather_plane(z_text)
    image_pre, keep, sent = tower_forward(mine, image_in, image_gain, image_up, image_down)
    image_resid, z_image = scattered_embed(mine, keep, sent, image_in, image_final)
    images = gather_column(z_image)

    *text_grads, keep, sent = pair_tile(images, near, left, right, far)
    image_dres = gather_rows(scatter_column(keep, sent, image_resid, image_final))
    keep, sent = tower_backward(image_dres, image_pre, image_up, image_down)
    image_grad, losses = input_grad(mine, image_in, image_gain, image_dres, keep, sent, True)

    text_dres = gather_rows(scatter_plane(text_grads, text_resid, text_final))
    keep, sent = tower_backward(text_dres, text_pre, text_up, text_down)
    text_grad = input_grad(mine, text_in, text_gain, text_dres, keep, sent, False)[0]
    return (image_grad, text_grad, losses.reshape(256))


def solution(mesh):
    placed = (
        P("dp", None),
        P("dp", None),
        P(),
        P(None, "mp"),
        P("mp", None),
        P(),
        P(),
        P(None, "mp"),
        P("mp", None),
        P(),
    )
    return jax.shard_map(
        on_device,
        mesh=mesh,
        in_specs=placed,
        out_specs=(P("dp", None), P("dp", None), P("dp")),
        check_vma=False,
    )
```

```python
import functools

import jax
import jax.numpy as jnp
import numpy as np
from jax import lax
from jax.experimental import pallas as pl
from jax.experimental.pallas import tpu as pltpu
from jax.sharding import PartitionSpec as P

epsilon = 1e-06
logit_scale = 10.0
logit_bias = -1.0
loss_scale = 32768.0
total_rows = 8192.0

WIDTH = 1408
HIDDEN = 1536
PACKED = 1536
BLOCK = 64
FF_STEP = 256
AXES = ("dp", "mp")
DIMS = (4, 4, 2, 2, 2)
bf16 = jnp.bfloat16
f32 = jnp.float32


def routes(move):
    pairs = []
    for source in range(128):
        y, x, z_hi, z_lo, core = (int(v) for v in np.unravel_index(source, DIMS))
        y, x, z, core = move(y, x, 2 * z_hi + z_lo, core)
        y, x, z = y % 4, x % 4, z % 4
        target = np.ravel_multi_index((y, x, z // 2, z % 2, core), DIMS)
        pairs.append((source, int(target)))
    return pairs


def first_ring(steps):
    return routes(lambda y, x, z, c: (y, x + steps, z, c) if c == 0 else (y + steps, x, z, c))


def second_ring(steps):
    return routes(lambda y, x, z, c: (y + steps, x, z, c) if c == 0 else (y, x + steps, z, c))


SIBLING = routes(lambda y, x, z, c: (y, x, z, 1 - c))
Z_PAIR = routes(lambda y, x, z, c: (y, x, z ^ 1, c))
Z_OUT = routes(lambda y, x, z, c: (y, x, z + 1 - 2 * c, c))
Z_BACK = routes(lambda y, x, z, c: (y, x, z - 1 + 2 * c, c))


def send(value, pairs):
    return lax.ppermute(value, AXES, pairs)


def contract(a, b, left, right):
    return lax.dot_general(a, b, (((left,), (right,)), ((), ())), preferred_element_type=f32)


def skipping(body, first, count, *refs):
    body(*refs[:first], *refs[first + count :])


def call(body, outs, args, scalar=None, after=(), flops=1, **options):
    specs = [pl.BlockSpec(memory_space=pltpu.VMEM) for _ in args]
    if after:
        count = len(args) + (scalar is not None)
        specs += [pl.BlockSpec(memory_space=pl.ANY) for _ in after]
        args = list(args) + list(after)
        body = functools.partial(skipping, body, count, len(after))
    if scalar is not None:
        specs = [pl.BlockSpec(memory_space=pltpu.SMEM)] + specs
        args = [scalar] + list(args)
    return pl.pallas_call(
        body,
        out_shape=outs,
        in_specs=specs,
        out_specs=[pl.BlockSpec(memory_space=pltpu.VMEM) for _ in outs],
        compiler_params=pltpu.CompilerParams(vmem_limit_bytes=30 << 20),
        cost_estimate=pl.CostEstimate(flops=flops, bytes_accessed=1, transcendentals=0),
        **options,
    )(*args)


def shape(rows, columns, kind):
    return jax.ShapeDtypeStruct((rows, columns), kind)


def centred(values):
    center = jnp.mean(values, axis=-1, keepdims=True)
    shifted = values - center
    variance = jnp.mean(shifted * shifted, axis=-1, keepdims=True)
    inverse = lax.rsqrt(variance + epsilon)
    return shifted * inverse, inverse


def centred_back(unit, inverse, d_unit):
    along = jnp.mean(d_unit * unit, axis=-1, keepdims=True)
    return inverse * (d_unit - jnp.mean(d_unit, axis=-1, keepdims=True) - unit * along)


def pack(out_ref, start, values, loss):
    rows = values.shape[0]
    column = lax.broadcasted_iota(jnp.int32, (rows, 128), 1)
    high = loss.astype(bf16).astype(f32)
    tail = jnp.where(column == 0, high, jnp.where(column == 1, loss - high, 0.0))
    out_ref[pl.ds(start, rows), 0:WIDTH] = values.astype(out_ref.dtype)
    out_ref[pl.ds(start, rows), WIDTH:PACKED] = tail.astype(out_ref.dtype)


def loss_of(tail):
    return jnp.sum(tail.astype(f32), axis=-1, keepdims=True)


SLOPE = 0.7978845608028654
CUBIC = 0.044715


def normed_rows(mine, x_ref, gain_ref, norm):
    gain = gain_ref[...].reshape(1, WIDTH)
    for place in range(4):
        start = pl.multiple_of((place ^ mine[0]) * BLOCK, BLOCK)
        unit, _ = centred(x_ref[pl.ds(start, BLOCK), :].astype(f32))
        norm[place * BLOCK : (place + 1) * BLOCK, :] = (unit * gain).astype(bf16)


def gelu(pre):
    return (0.5 * pre * (1.0 + jnp.tanh(SLOPE * (pre + CUBIC * pre * pre * pre)))).astype(bf16)


def forward_body(mine, x_ref, gain_ref, up_ref, down_ref, pre_ref, keep_ref, rest_ref, norm):
    normed_rows(mine, x_ref, gain_ref, norm)
    pre = contract(norm[...], up_ref[...], 1, 0)
    pre_ref[...] = pre
    part = contract(gelu(pre), down_ref[...], 1, 0)
    keep_ref[...] = part[0:128, :]
    rest_ref[...] = part[128:256, :]


UP_CUTS = ((0, 512), (512, 1024), (1024, 1408))
DOWN_CUTS = ((0, 768), (768, 1536))


def streamed_body(
    mine, x_ref, gain_ref, up_hbm, down_hbm, pre_ref, keep_ref, send_ref, norm, up_ref, down_ref, sems
):
    ups = [
        pltpu.make_async_copy(up_hbm.at[a:b], up_ref.at[a:b], sems.at[i])
        for i, (a, b) in enumerate(UP_CUTS)
    ]
    downs = [
        pltpu.make_async_copy(down_hbm.at[a:b], down_ref.at[a:b], sems.at[len(ups) + i])
        for i, (a, b) in enumerate(DOWN_CUTS)
    ]
    for copy in ups + downs:
        copy.start()
    normed_rows(mine, x_ref, gain_ref, norm)
    for copy, (a, b) in zip(ups, UP_CUTS):
        copy.wait()
        part = contract(norm[:, a:b], up_ref[a:b, :], 1, 0)
        pre_ref[...] = part if a == 0 else pre_ref[...] + part
    for copy, (a, b) in zip(downs, DOWN_CUTS):
        act = gelu(pre_ref[:, a:b])
        copy.wait()
        part = contract(act, down_ref[a:b, :], 1, 0)
        if a == 0:
            keep_ref[...] = part[0:128, :]
            rest = part[128:256, :]
        else:
            keep_ref[...] += part[0:128, :]
            send_ref[...] = (rest + part[128:256, :]).astype(bf16)


TOWER = dict(flops=4 * 256 * WIDTH * HIDDEN)


def tower_forward(mine, tokens, gain, up, down, after):
    return call(
        forward_body,
        [shape(256, HIDDEN, f32), shape(128, WIDTH, f32), shape(128, WIDTH, f32)],
        [tokens, gain, up, down],
        scalar=mine,
        after=after,
        scratch_shapes=[pltpu.VMEM((256, WIDTH), bf16)],
        **TOWER,
    )


def tower_streamed(mine, tokens, gain, up, down):
    vmem, hbm = pl.BlockSpec(memory_space=pltpu.VMEM), pl.BlockSpec(memory_space=pl.ANY)
    return pl.pallas_call(
        streamed_body,
        in_specs=[pl.BlockSpec(memory_space=pltpu.SMEM), vmem, vmem, hbm, hbm],
        out_specs=[vmem, vmem, vmem],
        out_shape=[shape(256, HIDDEN, f32), shape(128, WIDTH, f32), shape(128, WIDTH, bf16)],
        scratch_shapes=[
            pltpu.VMEM((256, WIDTH), bf16),
            pltpu.VMEM((WIDTH, HIDDEN), bf16),
            pltpu.VMEM((HIDDEN, WIDTH), bf16),
            pltpu.SemaphoreType.DMA((len(UP_CUTS) + len(DOWN_CUTS),)),
        ],
        compiler_params=pltpu.CompilerParams(vmem_limit_bytes=58 << 20),
        cost_estimate=pl.CostEstimate(
            flops=1, bytes_accessed=1, transcendentals=0
        ),
    )(mine, tokens, gain, up, down)


def backward_body(r0, r1, r2, r3, pre_ref, up_ref, down_ref, keep_ref, send_ref, given):
    for place, ref in enumerate((r0, r1, r2, r3)):
        given[place * BLOCK : (place + 1) * BLOCK, :] = ref[:, 0:WIDTH]
    d_act = contract(given[...], down_ref[...], 1, 1)
    pre = pre_ref[...]
    square = pre * pre
    curve = jnp.tanh(SLOPE * pre * (1.0 + CUBIC * square))
    slope = 0.5 * (1.0 + curve) + 0.5 * pre * (1.0 - curve * curve) * (
        SLOPE * (1.0 + 3.0 * CUBIC * square)
    )
    part = contract((d_act * slope).astype(bf16), up_ref[...], 1, 1)
    keep_ref[...] = part[0:128, :]
    send_ref[...] = part[128:256, :].astype(bf16)


def tower_backward(blocks, pre, up, down, after=()):
    return call(
        backward_body,
        [shape(128, WIDTH, f32), shape(128, WIDTH, bf16)],
        [*blocks, pre, up, down],
        after=after,
        scratch_shapes=[pltpu.VMEM((256, WIDTH), bf16)],
    )


def halve_body(keep_ref, got_ref, own_ref, send_ref):
    own_ref[...] = keep_ref[0:BLOCK, :] + got_ref[0:BLOCK, :].astype(f32)
    send_ref[...] = (keep_ref[BLOCK:128, :] + got_ref[BLOCK:128, :].astype(f32)).astype(bf16)


def embed_body(mine, own_ref, got_ref, x_ref, gain_ref, resid_ref, z_ref):
    start = pl.multiple_of(mine[0] * BLOCK, BLOCK)
    resid = own_ref[...] + got_ref[...].astype(f32) + x_ref[pl.ds(start, BLOCK), :].astype(f32)
    resid_ref[...] = resid
    normed = centred(resid)[0] * gain_ref[...].reshape(1, WIDTH)
    scale = lax.rsqrt(jnp.sum(normed * normed, axis=-1, keepdims=True) + epsilon)
    z_ref[...] = (normed * scale).astype(bf16)


def rounded_body(rest_ref, send_ref):
    send_ref[...] = rest_ref[...].astype(bf16)


def rounded(rest, after):
    return call(rounded_body, [shape(128, WIDTH, bf16)], [rest], after=after)[0]


def scatter_half(keep, sent):
    got = send(sent, SIBLING)
    return call(halve_body, [shape(BLOCK, WIDTH, f32), shape(BLOCK, WIDTH, bf16)], [keep, got])


def scattered_embed(mine, own, sent, tokens, final_gain, after=()):
    got = send(sent, Z_PAIR)
    return call(
        embed_body,
        [shape(BLOCK, WIDTH, f32), shape(BLOCK, WIDTH, bf16)],
        [own, got, tokens, final_gain],
        scalar=mine,
        after=after,
    )


def stack_body(*refs):
    for place, ref in enumerate(refs[:-1]):
        refs[-1][place * BLOCK : (place + 1) * BLOCK, :] = ref[...]


def stacked(*blocks, after=()):
    rows, columns = len(blocks) * BLOCK, blocks[0].shape[1]
    return call(stack_body, [shape(rows, columns, bf16)], list(blocks), after=after)[0]


def gather_plane(own, waited):
    before = send(own, first_ring(1))
    across = send(own, first_ring(2))
    after = send(own, first_ring(-1))
    near = (stacked(own, before, after=waited), stacked(after, across))
    left = [send(near[0], second_ring(1)), None]
    right = [None, send(near[1], second_ring(-1))]
    left[1] = send(near[1], second_ring(1))
    right[0] = send(near[0], second_ring(-1))
    far = (send(left[0], second_ring(1)), send(right[1], second_ring(-1)))
    return near, left, right, far


def gather_column(own):
    ahead = send(own, Z_OUT)
    behind = send(own, Z_BACK)
    across = send(ahead, Z_OUT)
    blocks = stacked(own, ahead, behind, across)
    return blocks, send(blocks, SIBLING)


def pair_chunk(images, texts, has_own):
    logits = logit_scale * contract(images, texts, 1, 1) + logit_bias
    grown = jnp.exp(logits)
    softplus = jnp.log1p(grown)
    share = grown / (1.0 + grown)
    if has_own:
        row = lax.broadcasted_iota(jnp.int32, logits.shape, 0)
        column = lax.broadcasted_iota(jnp.int32, logits.shape, 1)
        matched = (row == column) & (row < BLOCK)
        softplus = jnp.where(matched, softplus - logits, softplus)
        share = jnp.where(matched, share - 1.0, share)
    loss = jnp.sum(softplus, axis=1, keepdims=True) / total_rows
    pair_grad = (loss_scale / total_rows * share).astype(bf16)
    to_image = logit_scale * contract(pair_grad, texts, 1, 0)
    to_text = logit_scale * contract(pair_grad, images, 0, 0)
    return loss, to_image, to_text


def early_body(*refs):
    image_refs, refs = refs[:2], refs[2:]
    near0, near1, left0, left1, right0, right1 = refs[:6]
    image_ref, total_ref, loss_ref, near_ref, left_keep, left_send, right_send, right_keep = refs[6:14]
    texts = refs[14]
    for place, ref in enumerate(image_refs):
        image_ref[place * 256 : (place + 1) * 256, :] = ref[...]
    losses = 0.0
    for chunk, parts in enumerate(((near0, near1), (left0, left1), (right0, right1))):
        texts[0:128, :] = parts[0][...]
        texts[128:256, :] = parts[1][...]
        loss, to_image, to_text = pair_chunk(image_ref[...], texts[...], chunk == 0)
        losses = losses + loss
        if chunk == 0:
            total_ref[...] = to_image
            near_ref[...] = to_text
        else:
            total_ref[...] += to_image
            halves = (left_keep, left_send) if chunk == 1 else (right_send, right_keep)
            halves[0][...] = to_text[0:128, :].astype(halves[0].dtype)
            halves[1][...] = to_text[128:256, :].astype(halves[1].dtype)
    loss_ref[...] = jnp.broadcast_to(losses, (512, 128))


def late_body(image_ref, total_ref, loss_ref, far0, far1, far0_ref, far1_ref, keep_ref, send_ref, texts):
    texts[0:128, :] = far0[...]
    texts[128:256, :] = far1[...]
    loss, to_image, to_text = pair_chunk(image_ref[...], texts[...], False)
    far0_ref[...] = to_text[0:128, :].astype(bf16)
    far1_ref[...] = to_text[128:256, :].astype(bf16)
    loss = loss + loss_ref[:, 0:1]
    to_image = to_image + total_ref[...]
    pack(keep_ref, 0, to_image[0:256, :], loss[0:256, :])
    pack(send_ref, 0, to_image[256:512, :], loss[256:512, :])


def pair_tile(images, near, left, right, far):
    half32, half16 = shape(128, WIDTH, f32), shape(128, WIDTH, bf16)
    image, total, loss, near_grad, left_keep, left_send, right_send, right_keep = call(
        early_body,
        [shape(512, WIDTH, bf16), shape(512, WIDTH, f32), shape(512, 128, f32)]
        + [shape(256, WIDTH, f32), half32, half16, half16, half32],
        [*images, *near, *left, *right],
        scratch_shapes=[pltpu.VMEM((256, WIDTH), bf16)],
    )
    far0, far1, image_keep, image_send = call(
        late_body,
        [half16, half16, shape(256, PACKED, f32), shape(256, PACKED, bf16)],
        [image, total, loss, *far],
        scratch_shapes=[pltpu.VMEM((256, WIDTH), bf16)],
    )
    return near_grad, left_keep, left_send, right_send, right_keep, far0, far1, image_keep, image_send


def joined_body(keep_ref, got_ref, out_ref):
    out_ref[...] = (keep_ref[...] + got_ref[...].astype(f32)).astype(out_ref.dtype)


def near_body(near_ref, l0, l1, r0, r1, own_ref, before_ref, after_ref, across_ref):
    first = near_ref[0:128, :] + l0[...].astype(f32) + r0[...].astype(f32)
    second = near_ref[128:256, :] + l1[...].astype(f32) + r1[...].astype(f32)
    own_ref[...] = first[0:BLOCK, :]
    before_ref[...] = first[BLOCK:128, :].astype(bf16)
    after_ref[...] = second[0:BLOCK, :].astype(bf16)
    across_ref[...] = second[BLOCK:128, :].astype(bf16)


def head_back(resid, gain, d_embed):
    unit, inverse = centred(resid)
    normed = unit * gain
    scale = lax.rsqrt(jnp.sum(normed * normed, axis=-1, keepdims=True) + epsilon)
    along = jnp.sum(d_embed * normed, axis=-1, keepdims=True)
    d_normed = scale * d_embed - normed * (scale * scale * scale * along)
    return centred_back(unit, inverse, d_normed * gain)


def text_head_body(own_ref, before_ref, after_ref, across_ref, resid_ref, gain_ref, out_ref):
    d_embed = own_ref[...] + before_ref[...].astype(f32)
    d_embed = d_embed + after_ref[...].astype(f32) + across_ref[...].astype(f32)
    out_ref[...] = head_back(resid_ref[...], gain_ref[...].reshape(1, WIDTH), d_embed).astype(bf16)


def add_packed(values, loss, ref, start):
    rows = values.shape[0]
    return (
        values + ref[start : start + rows, 0:WIDTH].astype(f32),
        loss + loss_of(ref[start : start + rows, WIDTH:PACKED]),
    )


def packed_rows(ref, start, rows):
    return ref[start : start + rows, 0:WIDTH], loss_of(ref[start : start + rows, WIDTH:PACKED])


def column_first_body(keep_ref, got_ref, near_ref, across_ref):
    for place in range(3):
        values, loss = packed_rows(keep_ref, place * BLOCK, BLOCK)
        pack(near_ref, place * BLOCK, *add_packed(values, loss, got_ref, place * BLOCK))
    values, loss = packed_rows(keep_ref, 3 * BLOCK, BLOCK)
    pack(across_ref, 0, *add_packed(values, loss, got_ref, 3 * BLOCK))


def column_second_body(near_ref, got_ref, ahead_ref, behind_ref):
    values, loss = packed_rows(near_ref, BLOCK, BLOCK)
    pack(ahead_ref, 0, *add_packed(values, loss, got_ref, 0))
    pack(behind_ref, 0, *packed_rows(near_ref, 2 * BLOCK, BLOCK))


def image_head_body(near_ref, ahead_ref, behind_ref, resid_ref, gain_ref, out_ref):
    values, loss = packed_rows(near_ref, 0, BLOCK)
    values, loss = add_packed(values, loss, ahead_ref, 0)
    values, loss = add_packed(values, loss, behind_ref, 0)
    pack(out_ref, 0, head_back(resid_ref[...], gain_ref[...].reshape(1, WIDTH), values), loss)


def scatter_both(grads, keep, sent, text_head, image_head):
    near, left_keep, left_send, right_send, right_keep, far0, far1 = grads
    half16, block16 = shape(128, WIDTH, bf16), shape(BLOCK, WIDTH, bf16)
    packed16 = shape(BLOCK, PACKED, bf16)
    got = send(sent, SIBLING)
    got0 = send(far0, second_ring(-1))
    got1 = send(far1, second_ring(1))
    l1 = send(left_send, second_ring(-1))
    r0 = send(right_send, second_ring(1))
    column, across = call(column_first_body, [shape(3 * BLOCK, PACKED, f32), packed16], [keep, got])
    back = send(across, Z_BACK)

    l0 = call(joined_body, [half16], [left_keep, got0], after=[across])[0]
    r1 = call(joined_body, [half16], [right_keep, got1], after=[across])[0]
    l0 = send(l0, second_ring(-1))
    r1 = send(r1, second_ring(1))
    ahead, behind = call(column_second_body, [packed16, packed16], [column, back])
    got_ahead = send(ahead, Z_BACK)
    got_behind = send(behind, Z_OUT)

    own, before, after, across = call(
        near_body,
        [shape(BLOCK, WIDTH, f32), block16, block16, block16],
        [near, l0, l1, r0, r1],
        after=[ahead],
        flops=2 << 30,
    )
    across = send(across, first_ring(2))
    before = send(before, first_ring(-1))
    after = send(after, first_ring(1))
    image = call(image_head_body, [packed16], [column, got_ahead, got_behind, *image_head])[0]
    text = call(text_head_body, [block16], [own, before, after, across, *text_head], after=[image], flops=2 << 30)[0]
    return image, text


def gather_rows(own):
    other = send(own, Z_PAIR)
    return own, other, send(own, SIBLING), send(other, SIBLING)


def swapped_body(own_ref, got_ref, out_ref):
    own, got = own_ref[...].astype(f32), got_ref[...].astype(f32)
    out_ref[0:BLOCK, :] = (own[0:BLOCK, :] + got[BLOCK:128, :]).astype(bf16)
    out_ref[BLOCK:128, :] = (own[BLOCK:128, :] + got[0:BLOCK, :]).astype(bf16)


def grad_body(has_loss, mine, x_ref, gain_ref, r0, r1, r2, r3, own_ref, got_ref, out_ref, *loss_ref):
    losses = jnp.zeros((1, 256), f32)
    for place in range(4):
        target = place ^ mine[0]
        start = pl.multiple_of(target * BLOCK, BLOCK)
        unit, inverse = centred(x_ref[pl.ds(start, BLOCK), :].astype(f32))
        given, norms = (r0, r1, r2, r3)[place], own_ref if place < 2 else got_ref
        rows = slice((place % 2) * BLOCK, (place % 2 + 1) * BLOCK)
        d_norm = norms[rows, :].astype(f32)
        back = centred_back(unit, inverse, d_norm * gain_ref[...].reshape(1, WIDTH))
        out_ref[pl.ds(start, BLOCK), :] = given[:, 0:WIDTH].astype(f32) + back
        if has_loss:
            row = lax.broadcasted_iota(jnp.int32, (BLOCK, 256), 0)
            column = lax.broadcasted_iota(jnp.int32, (BLOCK, 256), 1)
            loss = loss_of(given[:, WIDTH:PACKED])
            spread = jnp.where(column == target * BLOCK + row, loss, 0.0)
            losses = losses + jnp.sum(spread, axis=0, keepdims=True)
    if has_loss:
        loss_ref[0][...] = losses


def input_grad(mine, tokens, gain, blocks, keep, sent, has_loss):
    half16 = shape(128, WIDTH, bf16)
    got = send(sent, SIBLING)
    half = call(joined_body, [half16], [keep, got])[0]
    got = send(half, Z_PAIR)
    own = call(swapped_body, [half16], [half, got])[0]
    got = send(own, SIBLING)
    outs = [shape(256, WIDTH, f32)] + ([shape(1, 256, f32)] if has_loss else [])
    return call(
        functools.partial(grad_body, has_loss),
        outs,
        [tokens, gain, *blocks, own, got],
        scalar=mine,
    )


def on_device(
    image_in,
    text_in,
    image_gain,
    image_up,
    image_down,
    image_final,
    text_gain,
    text_up,
    text_down,
    text_final,
):
    mp = lax.axis_index("mp")
    mine = (2 * (mp % 2) + mp // 2).astype(jnp.int32).reshape(1)

    text_pre, keep, sent = tower_streamed(mine, text_in, text_gain, text_up, text_down)
    own, sent = scatter_half(keep, sent)
    image_pre, image_keep, image_rest = tower_forward(
        mine, image_in, image_gain, image_up, image_down, [sent]
    )
    text_resid, z_text = scattered_embed(mine, own, sent, text_in, text_final, [image_rest])
    own, sent = scatter_half(image_keep, rounded(image_rest, [z_text]))
    near, left, right, far = gather_plane(z_text, [sent])
    image_resid, z_image = scattered_embed(mine, own, sent, image_in, image_final)
    images = gather_column(z_image)

    *text_grads, keep, sent = pair_tile(images, near, left, right, far)
    image_own, text_own = scatter_both(
        text_grads, keep, sent, (text_resid, text_final), (image_resid, image_final)
    )
    image_dres = gather_rows(image_own)
    text_dres = gather_rows(text_own)
    keep, sent = tower_backward(image_dres, image_pre, image_up, image_down)
    text_keep, text_sent = tower_backward(text_dres, text_pre, text_up, text_down, [sent])
    image_grad, losses = input_grad(mine, image_in, image_gain, image_dres, keep, sent, True)
    text_grad = input_grad(mine, text_in, text_gain, text_dres, text_keep, text_sent, False)[0]
    return (image_grad, text_grad, losses.reshape(256))


def solution(mesh):
    placed = (
        P("dp", None),
        P("dp", None),
        P(),
        P(None, "mp"),
        P("mp", None),
        P(),
        P(),
        P(None, "mp"),
        P("mp", None),
        P(),
    )
    return jax.shard_map(
        on_device,
        mesh=mesh,
        in_specs=placed,
        out_specs=(P("dp", None), P("dp", None), P("dp")),
        check_vma=False,
    )
```

```python
import functools

import jax
import jax.numpy as jnp
import numpy as np
from jax import lax
from jax.experimental import pallas as pl
from jax.experimental.pallas import tpu as pltpu
from jax.sharding import PartitionSpec as P

epsilon = 1e-06
logit_scale = 10.0
logit_bias = -1.0
loss_scale = 32768.0
total_rows = 8192.0

WIDTH = 1408
HIDDEN = 1536
PACKED = 1536
BLOCK = 64
FF_STEP = 256
AXES = ("dp", "mp")
DIMS = (4, 4, 2, 2, 2)
bf16 = jnp.bfloat16
f32 = jnp.float32


def routes(move):
    pairs = []
    for source in range(128):
        y, x, z_hi, z_lo, core = (int(v) for v in np.unravel_index(source, DIMS))
        y, x, z, core = move(y, x, 2 * z_hi + z_lo, core)
        y, x, z = y % 4, x % 4, z % 4
        target = np.ravel_multi_index((y, x, z // 2, z % 2, core), DIMS)
        pairs.append((source, int(target)))
    return pairs


def first_ring(steps):
    return routes(lambda y, x, z, c: (y, x + steps, z, c) if c == 0 else (y + steps, x, z, c))


def second_ring(steps):
    return routes(lambda y, x, z, c: (y + steps, x, z, c) if c == 0 else (y, x + steps, z, c))


SIBLING = routes(lambda y, x, z, c: (y, x, z, 1 - c))
Z_PAIR = routes(lambda y, x, z, c: (y, x, z ^ 1, c))
Z_OUT = routes(lambda y, x, z, c: (y, x, z + 1 - 2 * c, c))
Z_BACK = routes(lambda y, x, z, c: (y, x, z - 1 + 2 * c, c))


def send(value, pairs):
    return lax.ppermute(value, AXES, pairs)


def contract(a, b, left, right):
    return lax.dot_general(a, b, (((left,), (right,)), ((), ())), preferred_element_type=f32)


def skipping(body, first, count, *refs):
    body(*refs[:first], *refs[first + count :])


def call(body, outs, args, scalar=None, after=(), flops=1, **options):
    specs = [pl.BlockSpec(memory_space=pltpu.VMEM) for _ in args]
    if after:
        count = len(args) + (scalar is not None)
        specs += [pl.BlockSpec(memory_space=pl.ANY) for _ in after]
        args = list(args) + list(after)
        body = functools.partial(skipping, body, count, len(after))
    if scalar is not None:
        specs = [pl.BlockSpec(memory_space=pltpu.SMEM)] + specs
        args = [scalar] + list(args)
    return pl.pallas_call(
        body,
        out_shape=outs,
        in_specs=specs,
        out_specs=[pl.BlockSpec(memory_space=pltpu.VMEM) for _ in outs],
        compiler_params=pltpu.CompilerParams(vmem_limit_bytes=30 << 20),
        cost_estimate=pl.CostEstimate(flops=flops, bytes_accessed=1, transcendentals=0),
        **options,
    )(*args)


def shape(rows, columns, kind):
    return jax.ShapeDtypeStruct((rows, columns), kind)


def centred(values):
    center = jnp.mean(values, axis=-1, keepdims=True)
    shifted = values - center
    variance = jnp.mean(shifted * shifted, axis=-1, keepdims=True)
    inverse = lax.rsqrt(variance + epsilon)
    return shifted * inverse, inverse


def centred_back(unit, inverse, d_unit):
    along = jnp.mean(d_unit * unit, axis=-1, keepdims=True)
    return inverse * (d_unit - jnp.mean(d_unit, axis=-1, keepdims=True) - unit * along)


def pack(out_ref, start, values, loss):
    rows = values.shape[0]
    column = lax.broadcasted_iota(jnp.int32, (rows, 128), 1)
    high = loss.astype(bf16).astype(f32)
    tail = jnp.where(column == 0, high, jnp.where(column == 1, loss - high, 0.0))
    out_ref[pl.ds(start, rows), 0:WIDTH] = values.astype(out_ref.dtype)
    out_ref[pl.ds(start, rows), WIDTH:PACKED] = tail.astype(out_ref.dtype)


def loss_of(tail):
    return jnp.sum(tail.astype(f32), axis=-1, keepdims=True)


SLOPE = 0.7978845608028654
CUBIC = 0.044715


def normed_rows(mine, x_ref, gain_ref, norm):
    gain = gain_ref[...].reshape(1, WIDTH)
    for place in range(4):
        start = pl.multiple_of((place ^ mine[0]) * BLOCK, BLOCK)
        unit, _ = centred(x_ref[pl.ds(start, BLOCK), :].astype(f32))
        norm[place * BLOCK : (place + 1) * BLOCK, :] = (unit * gain).astype(bf16)


def gelu(pre):
    return (0.5 * pre * (1.0 + jnp.tanh(SLOPE * (pre + CUBIC * pre * pre * pre)))).astype(bf16)


def forward_body(mine, x_ref, gain_ref, up_ref, down_ref, pre_ref, keep_ref, rest_ref, norm):
    normed_rows(mine, x_ref, gain_ref, norm)
    pre = contract(norm[...], up_ref[...], 1, 0)
    pre_ref[...] = pre
    part = contract(gelu(pre), down_ref[...], 1, 0)
    keep_ref[...] = part[0:128, :]
    rest_ref[...] = part[128:256, :]


UP_CUTS = ((0, 512), (512, 1024), (1024, 1408))
DOWN_CUTS = ((0, 768), (768, 1536))


def streamed_body(
    mine, x_ref, gain_ref, up_hbm, down_hbm, pre_ref, keep_ref, send_ref, norm, up_ref, down_ref, sems
):
    ups = [
        pltpu.make_async_copy(up_hbm.at[a:b], up_ref.at[a:b], sems.at[i])
        for i, (a, b) in enumerate(UP_CUTS)
    ]
    downs = [
        pltpu.make_async_copy(down_hbm.at[a:b], down_ref.at[a:b], sems.at[len(ups) + i])
        for i, (a, b) in enumerate(DOWN_CUTS)
    ]
    for copy in ups + downs:
        copy.start()
    normed_rows(mine, x_ref, gain_ref, norm)
    for copy, (a, b) in zip(ups, UP_CUTS):
        copy.wait()
        part = contract(norm[:, a:b], up_ref[a:b, :], 1, 0)
        pre_ref[...] = part if a == 0 else pre_ref[...] + part
    for copy, (a, b) in zip(downs, DOWN_CUTS):
        act = gelu(pre_ref[:, a:b])
        copy.wait()
        part = contract(act, down_ref[a:b, :], 1, 0)
        if a == 0:
            keep_ref[...] = part[0:128, :]
            rest = part[128:256, :]
        else:
            keep_ref[...] += part[0:128, :]
            send_ref[...] = (rest + part[128:256, :]).astype(bf16)


TOWER = dict(flops=4 * 256 * WIDTH * HIDDEN)


def tower_forward(mine, tokens, gain, up, down, after):
    return call(
        forward_body,
        [shape(256, HIDDEN, f32), shape(128, WIDTH, f32), shape(128, WIDTH, f32)],
        [tokens, gain, up, down],
        scalar=mine,
        after=after,
        scratch_shapes=[pltpu.VMEM((256, WIDTH), bf16)],
        **TOWER,
    )


def tower_streamed(mine, tokens, gain, up, down):
    vmem, hbm = pl.BlockSpec(memory_space=pltpu.VMEM), pl.BlockSpec(memory_space=pl.ANY)
    return pl.pallas_call(
        streamed_body,
        in_specs=[pl.BlockSpec(memory_space=pltpu.SMEM), vmem, vmem, hbm, hbm],
        out_specs=[vmem, vmem, vmem],
        out_shape=[shape(256, HIDDEN, f32), shape(128, WIDTH, f32), shape(128, WIDTH, bf16)],
        scratch_shapes=[
            pltpu.VMEM((256, WIDTH), bf16),
            pltpu.VMEM((WIDTH, HIDDEN), bf16),
            pltpu.VMEM((HIDDEN, WIDTH), bf16),
            pltpu.SemaphoreType.DMA((len(UP_CUTS) + len(DOWN_CUTS),)),
        ],
        compiler_params=pltpu.CompilerParams(vmem_limit_bytes=46 << 20),
        cost_estimate=pl.CostEstimate(
            flops=1, bytes_accessed=1, transcendentals=0
        ),
    )(mine, tokens, gain, up, down)


def backward_body(r0, r1, r2, r3, pre_ref, up_ref, down_ref, keep_ref, send_ref, given):
    for place, ref in enumerate((r0, r1, r2, r3)):
        given[place * BLOCK : (place + 1) * BLOCK, :] = ref[:, 0:WIDTH]
    d_act = contract(given[...], down_ref[...], 1, 1)
    pre = pre_ref[...]
    square = pre * pre
    curve = jnp.tanh(SLOPE * pre * (1.0 + CUBIC * square))
    slope = 0.5 * (1.0 + curve) + 0.5 * pre * (1.0 - curve * curve) * (
        SLOPE * (1.0 + 3.0 * CUBIC * square)
    )
    part = contract((d_act * slope).astype(bf16), up_ref[...], 1, 1)
    keep_ref[...] = part[0:128, :]
    send_ref[...] = part[128:256, :].astype(bf16)


def tower_backward(blocks, pre, up, down, after=()):
    return call(
        backward_body,
        [shape(128, WIDTH, f32), shape(128, WIDTH, bf16)],
        [*blocks, pre, up, down],
        after=after,
        scratch_shapes=[pltpu.VMEM((256, WIDTH), bf16)],
    )


def halve_body(keep_ref, got_ref, own_ref, send_ref):
    own_ref[...] = keep_ref[0:BLOCK, :] + got_ref[0:BLOCK, :].astype(f32)
    send_ref[...] = (keep_ref[BLOCK:128, :] + got_ref[BLOCK:128, :].astype(f32)).astype(bf16)


def embed_body(mine, own_ref, got_ref, x_ref, gain_ref, resid_ref, z_ref):
    start = pl.multiple_of(mine[0] * BLOCK, BLOCK)
    resid = own_ref[...] + got_ref[...].astype(f32) + x_ref[pl.ds(start, BLOCK), :].astype(f32)
    resid_ref[...] = resid
    normed = centred(resid)[0] * gain_ref[...].reshape(1, WIDTH)
    scale = lax.rsqrt(jnp.sum(normed * normed, axis=-1, keepdims=True) + epsilon)
    z_ref[...] = (normed * scale).astype(bf16)


def rounded_body(rest_ref, send_ref):
    send_ref[...] = rest_ref[...].astype(bf16)


def rounded(rest, after):
    return call(rounded_body, [shape(128, WIDTH, bf16)], [rest], after=after)[0]


def scatter_half(keep, sent):
    got = send(sent, SIBLING)
    return call(halve_body, [shape(BLOCK, WIDTH, f32), shape(BLOCK, WIDTH, bf16)], [keep, got])


def scattered_embed(mine, own, sent, tokens, final_gain, after=()):
    got = send(sent, Z_PAIR)
    return call(
        embed_body,
        [shape(BLOCK, WIDTH, f32), shape(BLOCK, WIDTH, bf16)],
        [own, got, tokens, final_gain],
        scalar=mine,
        after=after,
    )


def stack_body(*refs):
    for place, ref in enumerate(refs[:-1]):
        refs[-1][place * BLOCK : (place + 1) * BLOCK, :] = ref[...]


def stacked(*blocks, after=()):
    rows, columns = len(blocks) * BLOCK, blocks[0].shape[1]
    return call(stack_body, [shape(rows, columns, bf16)], list(blocks), after=after)[0]


def gather_plane(own, waited):
    before = send(own, first_ring(1))
    across = send(own, first_ring(2))
    after = send(own, first_ring(-1))
    near = (stacked(own, before, after=waited), stacked(after, across))
    left = [send(near[0], second_ring(1)), None]
    right = [None, send(near[1], second_ring(-1))]
    left[1] = send(near[1], second_ring(1))
    right[0] = send(near[0], second_ring(-1))
    far = (send(left[0], second_ring(1)), send(right[1], second_ring(-1)))
    return near, left, right, far


def gather_column(own):
    ahead = send(own, Z_OUT)
    behind = send(own, Z_BACK)
    across = send(ahead, Z_OUT)
    blocks = stacked(own, ahead, behind, across)
    return blocks, send(blocks, SIBLING)


def pair_chunk(images, texts, has_own):
    logits = logit_scale * contract(images, texts, 1, 1) + logit_bias
    grown = jnp.exp(logits)
    softplus = jnp.log1p(grown)
    share = grown / (1.0 + grown)
    if has_own:
        row = lax.broadcasted_iota(jnp.int32, logits.shape, 0)
        column = lax.broadcasted_iota(jnp.int32, logits.shape, 1)
        matched = (row == column) & (row < BLOCK)
        softplus = jnp.where(matched, softplus - logits, softplus)
        share = jnp.where(matched, share - 1.0, share)
    loss = jnp.sum(softplus, axis=1, keepdims=True) / total_rows
    pair_grad = (loss_scale / total_rows * share).astype(bf16)
    to_image = logit_scale * contract(pair_grad, texts, 1, 0)
    to_text = logit_scale * contract(pair_grad, images, 0, 0)
    return loss, to_image, to_text


def early_body(*refs):
    image_refs, text_refs = refs[:2], refs[2:8]
    image_ref, total_ref, loss_ref, near_ref, left_keep, left_send, right_send, right_keep = refs[8:16]
    texts = refs[16]
    for place, ref in enumerate(image_refs):
        image_ref[place * 256 : (place + 1) * 256, :] = ref[...]
    for place, ref in enumerate(text_refs):
        texts[place * 128 : (place + 1) * 128, :] = ref[...]
    loss, to_image, to_text = pair_chunk(image_ref[...], texts[...], True)
    total_ref[...] = to_image
    near_ref[...] = to_text[0:256, :]
    for place, ref in enumerate((left_keep, left_send, right_send, right_keep)):
        ref[...] = to_text[256 + place * 128 : 384 + place * 128, :].astype(ref.dtype)
    loss_ref[...] = jnp.broadcast_to(loss, (512, 128))


def late_body(image_ref, total_ref, loss_ref, far0, far1, far0_ref, far1_ref, keep_ref, send_ref, texts):
    texts[0:128, :] = far0[...]
    texts[128:256, :] = far1[...]
    loss, to_image, to_text = pair_chunk(image_ref[...], texts[...], False)
    far0_ref[...] = to_text[0:128, :].astype(bf16)
    far1_ref[...] = to_text[128:256, :].astype(bf16)
    loss = loss + loss_ref[:, 0:1]
    to_image = to_image + total_ref[...]
    pack(keep_ref, 0, to_image[0:256, :], loss[0:256, :])
    pack(send_ref, 0, to_image[256:512, :], loss[256:512, :])


def pair_tile(images, near, left, right, far):
    half32, half16 = shape(128, WIDTH, f32), shape(128, WIDTH, bf16)
    image, total, loss, near_grad, left_keep, left_send, right_send, right_keep = call(
        early_body,
        [shape(512, WIDTH, bf16), shape(512, WIDTH, f32), shape(512, 128, f32)]
        + [shape(256, WIDTH, f32), half32, half16, half16, half32],
        [*images, *near, *left, *right],
        scratch_shapes=[pltpu.VMEM((768, WIDTH), bf16)],
    )
    far0, far1, image_keep, image_send = call(
        late_body,
        [half16, half16, shape(256, PACKED, f32), shape(256, PACKED, bf16)],
        [image, total, loss, *far],
        scratch_shapes=[pltpu.VMEM((256, WIDTH), bf16)],
    )
    return near_grad, left_keep, left_send, right_send, right_keep, far0, far1, image_keep, image_send


def joined_body(keep_ref, got_ref, out_ref):
    out_ref[...] = (keep_ref[...] + got_ref[...].astype(f32)).astype(out_ref.dtype)


def near_body(near_ref, l0, l1, r0, r1, own_ref, before_ref, after_ref, across_ref):
    first = near_ref[0:128, :] + l0[...].astype(f32) + r0[...].astype(f32)
    second = near_ref[128:256, :] + l1[...].astype(f32) + r1[...].astype(f32)
    own_ref[...] = first[0:BLOCK, :]
    before_ref[...] = first[BLOCK:128, :].astype(bf16)
    after_ref[...] = second[0:BLOCK, :].astype(bf16)
    across_ref[...] = second[BLOCK:128, :].astype(bf16)


def head_back(resid, gain, d_embed):
    unit, inverse = centred(resid)
    normed = unit * gain
    scale = lax.rsqrt(jnp.sum(normed * normed, axis=-1, keepdims=True) + epsilon)
    along = jnp.sum(d_embed * normed, axis=-1, keepdims=True)
    d_normed = scale * d_embed - normed * (scale * scale * scale * along)
    return centred_back(unit, inverse, d_normed * gain)


def text_head_body(own_ref, before_ref, after_ref, across_ref, resid_ref, gain_ref, out_ref):
    d_embed = own_ref[...] + before_ref[...].astype(f32)
    d_embed = d_embed + after_ref[...].astype(f32) + across_ref[...].astype(f32)
    out_ref[...] = head_back(resid_ref[...], gain_ref[...].reshape(1, WIDTH), d_embed).astype(bf16)


def add_packed(values, loss, ref, start):
    rows = values.shape[0]
    return (
        values + ref[start : start + rows, 0:WIDTH].astype(f32),
        loss + loss_of(ref[start : start + rows, WIDTH:PACKED]),
    )


def packed_rows(ref, start, rows):
    return ref[start : start + rows, 0:WIDTH], loss_of(ref[start : start + rows, WIDTH:PACKED])


def column_first_body(keep_ref, got_ref, near_ref, across_ref):
    for place in range(3):
        values, loss = packed_rows(keep_ref, place * BLOCK, BLOCK)
        pack(near_ref, place * BLOCK, *add_packed(values, loss, got_ref, place * BLOCK))
    values, loss = packed_rows(keep_ref, 3 * BLOCK, BLOCK)
    pack(across_ref, 0, *add_packed(values, loss, got_ref, 3 * BLOCK))


def column_second_body(near_ref, got_ref, ahead_ref, behind_ref):
    values, loss = packed_rows(near_ref, BLOCK, BLOCK)
    pack(ahead_ref, 0, *add_packed(values, loss, got_ref, 0))
    pack(behind_ref, 0, *packed_rows(near_ref, 2 * BLOCK, BLOCK))


def image_head_body(near_ref, ahead_ref, behind_ref, resid_ref, gain_ref, out_ref):
    values, loss = packed_rows(near_ref, 0, BLOCK)
    values, loss = add_packed(values, loss, ahead_ref, 0)
    values, loss = add_packed(values, loss, behind_ref, 0)
    pack(out_ref, 0, head_back(resid_ref[...], gain_ref[...].reshape(1, WIDTH), values), loss)


def scatter_both(grads, keep, sent, text_head, image_head):
    near, left_keep, left_send, right_send, right_keep, far0, far1 = grads
    half16, block16 = shape(128, WIDTH, bf16), shape(BLOCK, WIDTH, bf16)
    packed16 = shape(BLOCK, PACKED, bf16)
    got = send(sent, SIBLING)
    got0 = send(far0, second_ring(-1))
    got1 = send(far1, second_ring(1))
    l1 = send(left_send, second_ring(-1))
    r0 = send(right_send, second_ring(1))
    column, across = call(column_first_body, [shape(3 * BLOCK, PACKED, f32), packed16], [keep, got])
    back = send(across, Z_BACK)

    l0 = call(joined_body, [half16], [left_keep, got0], after=[across])[0]
    r1 = call(joined_body, [half16], [right_keep, got1], after=[across])[0]
    l0 = send(l0, second_ring(-1))
    r1 = send(r1, second_ring(1))
    ahead, behind = call(column_second_body, [packed16, packed16], [column, back])
    got_ahead = send(ahead, Z_BACK)
    got_behind = send(behind, Z_OUT)

    own, before, after, across = call(
        near_body,
        [shape(BLOCK, WIDTH, f32), block16, block16, block16],
        [near, l0, l1, r0, r1],
        after=[ahead],
        flops=2 << 30,
    )
    across = send(across, first_ring(2))
    before = send(before, first_ring(-1))
    after = send(after, first_ring(1))
    image = call(image_head_body, [packed16], [column, got_ahead, got_behind, *image_head])[0]
    text = call(text_head_body, [block16], [own, before, after, across, *text_head], after=[image], flops=2 << 30)[0]
    return image, text


def gather_rows(own):
    other = send(own, Z_PAIR)
    return own, other, send(own, SIBLING), send(other, SIBLING)


def swapped_body(own_ref, got_ref, out_ref):
    own, got = own_ref[...].astype(f32), got_ref[...].astype(f32)
    out_ref[0:BLOCK, :] = (own[0:BLOCK, :] + got[BLOCK:128, :]).astype(bf16)
    out_ref[BLOCK:128, :] = (own[BLOCK:128, :] + got[0:BLOCK, :]).astype(bf16)


def grad_body(has_loss, mine, x_ref, gain_ref, r0, r1, r2, r3, own_ref, got_ref, out_ref, *loss_ref):
    losses = jnp.zeros((1, 256), f32)
    for place in range(4):
        target = place ^ mine[0]
        start = pl.multiple_of(target * BLOCK, BLOCK)
        unit, inverse = centred(x_ref[pl.ds(start, BLOCK), :].astype(f32))
        given, norms = (r0, r1, r2, r3)[place], own_ref if place < 2 else got_ref
        rows = slice((place % 2) * BLOCK, (place % 2 + 1) * BLOCK)
        d_norm = norms[rows, :].astype(f32)
        back = centred_back(unit, inverse, d_norm * gain_ref[...].reshape(1, WIDTH))
        out_ref[pl.ds(start, BLOCK), :] = given[:, 0:WIDTH].astype(f32) + back
        if has_loss:
            row = lax.broadcasted_iota(jnp.int32, (BLOCK, 256), 0)
            column = lax.broadcasted_iota(jnp.int32, (BLOCK, 256), 1)
            loss = loss_of(given[:, WIDTH:PACKED])
            spread = jnp.where(column == target * BLOCK + row, loss, 0.0)
            losses = losses + jnp.sum(spread, axis=0, keepdims=True)
    if has_loss:
        loss_ref[0][...] = losses


def input_grad(mine, tokens, gain, blocks, keep, sent, has_loss):
    half16 = shape(128, WIDTH, bf16)
    got = send(sent, SIBLING)
    half = call(joined_body, [half16], [keep, got])[0]
    got = send(half, Z_PAIR)
    own = call(swapped_body, [half16], [half, got])[0]
    got = send(own, SIBLING)
    outs = [shape(256, WIDTH, f32)] + ([shape(1, 256, f32)] if has_loss else [])
    return call(
        functools.partial(grad_body, has_loss),
        outs,
        [tokens, gain, *blocks, own, got],
        scalar=mine,
    )


def on_device(
    image_in,
    text_in,
    image_gain,
    image_up,
    image_down,
    image_final,
    text_gain,
    text_up,
    text_down,
    text_final,
):
    mp = lax.axis_index("mp")
    mine = (2 * (mp % 2) + mp // 2).astype(jnp.int32).reshape(1)

    text_pre, keep, sent = tower_streamed(mine, text_in, text_gain, text_up, text_down)
    own, sent = scatter_half(keep, sent)
    image_pre, image_keep, image_rest = tower_forward(
        mine, image_in, image_gain, image_up, image_down, [sent]
    )
    text_resid, z_text = scattered_embed(mine, own, sent, text_in, text_final, [image_rest])
    own, sent = scatter_half(image_keep, rounded(image_rest, [z_text]))
    near, left, right, far = gather_plane(z_text, [sent])
    image_resid, z_image = scattered_embed(mine, own, sent, image_in, image_final)
    images = gather_column(z_image)

    *text_grads, keep, sent = pair_tile(images, near, left, right, far)
    image_own, text_own = scatter_both(
        text_grads, keep, sent, (text_resid, text_final), (image_resid, image_final)
    )
    image_dres = gather_rows(image_own)
    text_dres = gather_rows(text_own)
    keep, sent = tower_backward(image_dres, image_pre, image_up, image_down)
    text_keep, text_sent = tower_backward(text_dres, text_pre, text_up, text_down, [sent])
    image_grad, losses = input_grad(mine, image_in, image_gain, image_dres, keep, sent, True)
    text_grad = input_grad(mine, text_in, text_gain, text_dres, text_keep, text_sent, False)[0]
    return (image_grad, text_grad, losses.reshape(256))


def solution(mesh):
    placed = (
        P("dp", None),
        P("dp", None),
        P(),
        P(None, "mp"),
        P("mp", None),
        P(),
        P(),
        P(None, "mp"),
        P("mp", None),
        P(),
    )
    return jax.shard_map(
        on_device,
        mesh=mesh,
        in_specs=placed,
        out_specs=(P("dp", None), P("dp", None), P("dp")),
        check_vma=False,
    )
```

```python
import functools

import jax
import jax.numpy as jnp
import numpy as np
from jax import lax
from jax.experimental import pallas as pl
from jax.experimental.pallas import tpu as pltpu
from jax.sharding import PartitionSpec as P

epsilon = 1e-06
logit_scale = 10.0
logit_bias = -1.0
loss_scale = 32768.0
total_rows = 8192.0

WIDTH = 1408
HIDDEN = 1536
PACKED = 1536
BLOCK = 64
FF_STEP = 256
AXES = ("dp", "mp")
DIMS = (4, 4, 2, 2, 2)
bf16 = jnp.bfloat16
f32 = jnp.float32


def routes(move):
    pairs = []
    for source in range(128):
        y, x, z_hi, z_lo, core = (int(v) for v in np.unravel_index(source, DIMS))
        y, x, z, core = move(y, x, 2 * z_hi + z_lo, core)
        y, x, z = y % 4, x % 4, z % 4
        target = np.ravel_multi_index((y, x, z // 2, z % 2, core), DIMS)
        pairs.append((source, int(target)))
    return pairs


def first_ring(steps):
    return routes(lambda y, x, z, c: (y, x + steps, z, c) if c == 0 else (y + steps, x, z, c))


def second_ring(steps):
    return routes(lambda y, x, z, c: (y + steps, x, z, c) if c == 0 else (y, x + steps, z, c))


SIBLING = routes(lambda y, x, z, c: (y, x, z, 1 - c))
Z_PAIR = routes(lambda y, x, z, c: (y, x, z ^ 1, c))
Z_OUT = routes(lambda y, x, z, c: (y, x, z + 1 - 2 * c, c))
Z_BACK = routes(lambda y, x, z, c: (y, x, z - 1 + 2 * c, c))


def send(value, pairs):
    return lax.ppermute(value, AXES, pairs)


def contract(a, b, left, right):
    return lax.dot_general(a, b, (((left,), (right,)), ((), ())), preferred_element_type=f32)


def skipping(body, first, count, *refs):
    body(*refs[:first], *refs[first + count :])


def call(body, outs, args, scalar=None, after=(), flops=1, **options):
    specs = [pl.BlockSpec(memory_space=pltpu.VMEM) for _ in args]
    if after:
        count = len(args) + (scalar is not None)
        specs += [pl.BlockSpec(memory_space=pl.ANY) for _ in after]
        args = list(args) + list(after)
        body = functools.partial(skipping, body, count, len(after))
    if scalar is not None:
        specs = [pl.BlockSpec(memory_space=pltpu.SMEM)] + specs
        args = [scalar] + list(args)
    return pl.pallas_call(
        body,
        out_shape=outs,
        in_specs=specs,
        out_specs=[pl.BlockSpec(memory_space=pltpu.VMEM) for _ in outs],
        compiler_params=pltpu.CompilerParams(vmem_limit_bytes=30 << 20),
        cost_estimate=pl.CostEstimate(flops=flops, bytes_accessed=1, transcendentals=0),
        **options,
    )(*args)


def shape(rows, columns, kind):
    return jax.ShapeDtypeStruct((rows, columns), kind)


def centred(values):
    center = jnp.mean(values, axis=-1, keepdims=True)
    shifted = values - center
    variance = jnp.mean(shifted * shifted, axis=-1, keepdims=True)
    inverse = lax.rsqrt(variance + epsilon)
    return shifted * inverse, inverse


def centred_back(unit, inverse, d_unit):
    along = jnp.mean(d_unit * unit, axis=-1, keepdims=True)
    return inverse * (d_unit - jnp.mean(d_unit, axis=-1, keepdims=True) - unit * along)


def pack(out_ref, start, values, loss):
    rows = values.shape[0]
    column = lax.broadcasted_iota(jnp.int32, (rows, 128), 1)
    high = loss.astype(bf16).astype(f32)
    tail = jnp.where(column == 0, high, jnp.where(column == 1, loss - high, 0.0))
    out_ref[pl.ds(start, rows), 0:WIDTH] = values.astype(out_ref.dtype)
    out_ref[pl.ds(start, rows), WIDTH:PACKED] = tail.astype(out_ref.dtype)


def loss_of(tail):
    return jnp.sum(tail.astype(f32), axis=-1, keepdims=True)


SLOPE = 0.7978845608028654
CUBIC = 0.044715


def normed_rows(mine, x_ref, gain_ref, norm):
    gain = gain_ref[...].reshape(1, WIDTH)
    for place in range(4):
        start = pl.multiple_of((place ^ mine[0]) * BLOCK, BLOCK)
        unit, _ = centred(x_ref[pl.ds(start, BLOCK), :].astype(f32))
        norm[place * BLOCK : (place + 1) * BLOCK, :] = (unit * gain).astype(bf16)


def gelu(pre):
    return (0.5 * pre * (1.0 + jnp.tanh(SLOPE * (pre + CUBIC * pre * pre * pre)))).astype(bf16)


def forward_body(mine, x_ref, gain_ref, up_ref, down_ref, pre_ref, keep_ref, rest_ref, norm):
    normed_rows(mine, x_ref, gain_ref, norm)
    pre = contract(norm[...], up_ref[...], 1, 0)
    pre_ref[...] = pre
    part = contract(gelu(pre), down_ref[...], 1, 0)
    keep_ref[...] = part[0:128, :]
    rest_ref[...] = part[128:256, :]


UP_CUTS = ((0, 512), (512, 1024), (1024, 1408))
DOWN_CUTS = ((0, 768), (768, 1536))


def streamed_body(
    mine, x_ref, gain_ref, up_hbm, down_hbm, pre_ref, keep_ref, send_ref, norm, up_ref, down_ref, sems
):
    ups = [
        pltpu.make_async_copy(up_hbm.at[a:b], up_ref.at[a:b], sems.at[i])
        for i, (a, b) in enumerate(UP_CUTS)
    ]
    downs = [
        pltpu.make_async_copy(down_hbm.at[a:b], down_ref.at[a:b], sems.at[len(ups) + i])
        for i, (a, b) in enumerate(DOWN_CUTS)
    ]
    for copy in ups + downs:
        copy.start()
    normed_rows(mine, x_ref, gain_ref, norm)
    for copy, (a, b) in zip(ups, UP_CUTS):
        copy.wait()
        part = contract(norm[:, a:b], up_ref[a:b, :], 1, 0)
        pre_ref[...] = part if a == 0 else pre_ref[...] + part
    for copy, (a, b) in zip(downs, DOWN_CUTS):
        act = gelu(pre_ref[:, a:b])
        copy.wait()
        part = contract(act, down_ref[a:b, :], 1, 0)
        if a == 0:
            keep_ref[...] = part[0:128, :]
            rest = part[128:256, :]
        else:
            keep_ref[...] += part[0:128, :]
            send_ref[...] = (rest + part[128:256, :]).astype(bf16)


TOWER = dict(flops=4 * 256 * WIDTH * HIDDEN)


def tower_forward(mine, tokens, gain, up, down, after):
    return call(
        forward_body,
        [shape(256, HIDDEN, f32), shape(128, WIDTH, f32), shape(128, WIDTH, f32)],
        [tokens, gain, up, down],
        scalar=mine,
        after=after,
        scratch_shapes=[pltpu.VMEM((256, WIDTH), bf16)],
        **TOWER,
    )


def tower_streamed(mine, tokens, gain, up, down):
    vmem, hbm = pl.BlockSpec(memory_space=pltpu.VMEM), pl.BlockSpec(memory_space=pl.ANY)
    return pl.pallas_call(
        streamed_body,
        in_specs=[pl.BlockSpec(memory_space=pltpu.SMEM), vmem, vmem, hbm, hbm],
        out_specs=[vmem, vmem, vmem],
        out_shape=[shape(256, HIDDEN, f32), shape(128, WIDTH, f32), shape(128, WIDTH, bf16)],
        scratch_shapes=[
            pltpu.VMEM((256, WIDTH), bf16),
            pltpu.VMEM((WIDTH, HIDDEN), bf16),
            pltpu.VMEM((HIDDEN, WIDTH), bf16),
            pltpu.SemaphoreType.DMA((len(UP_CUTS) + len(DOWN_CUTS),)),
        ],
        compiler_params=pltpu.CompilerParams(vmem_limit_bytes=46 << 20),
        cost_estimate=pl.CostEstimate(
            flops=1, bytes_accessed=1, transcendentals=0
        ),
    )(mine, tokens, gain, up, down)


def backward_body(r0, r1, r2, r3, pre_ref, up_ref, down_ref, keep_ref, send_ref, given):
    for place, ref in enumerate((r0, r1, r2, r3)):
        given[place * BLOCK : (place + 1) * BLOCK, :] = ref[:, 0:WIDTH]
    d_act = contract(given[...], down_ref[...], 1, 1)
    pre = pre_ref[...]
    square = pre * pre
    curve = jnp.tanh(SLOPE * pre * (1.0 + CUBIC * square))
    slope = 0.5 * (1.0 + curve) + 0.5 * pre * (1.0 - curve * curve) * (
        SLOPE * (1.0 + 3.0 * CUBIC * square)
    )
    part = contract((d_act * slope).astype(bf16), up_ref[...], 1, 1)
    keep_ref[...] = part[0:128, :]
    send_ref[...] = part[128:256, :].astype(bf16)


def tower_backward(blocks, pre, up, down, after=()):
    return call(
        backward_body,
        [shape(128, WIDTH, f32), shape(128, WIDTH, bf16)],
        [*blocks, pre, up, down],
        after=after,
        scratch_shapes=[pltpu.VMEM((256, WIDTH), bf16)],
    )


def halve_body(keep_ref, got_ref, own_ref, send_ref):
    own_ref[...] = keep_ref[0:BLOCK, :] + got_ref[0:BLOCK, :].astype(f32)
    send_ref[...] = (keep_ref[BLOCK:128, :] + got_ref[BLOCK:128, :].astype(f32)).astype(bf16)


def embed_body(mine, own_ref, got_ref, x_ref, gain_ref, resid_ref, z_ref):
    start = pl.multiple_of(mine[0] * BLOCK, BLOCK)
    resid = own_ref[...] + got_ref[...].astype(f32) + x_ref[pl.ds(start, BLOCK), :].astype(f32)
    resid_ref[...] = resid
    normed = centred(resid)[0] * gain_ref[...].reshape(1, WIDTH)
    scale = lax.rsqrt(jnp.sum(normed * normed, axis=-1, keepdims=True) + epsilon)
    z_ref[...] = (normed * scale).astype(bf16)


def rounded_body(rest_ref, send_ref):
    send_ref[...] = rest_ref[...].astype(bf16)


def rounded(rest, after):
    return call(rounded_body, [shape(128, WIDTH, bf16)], [rest], after=after)[0]


def scatter_half(keep, sent):
    got = send(sent, SIBLING)
    return call(halve_body, [shape(BLOCK, WIDTH, f32), shape(BLOCK, WIDTH, bf16)], [keep, got])


def scattered_embed(mine, own, sent, tokens, final_gain, after=()):
    got = send(sent, Z_PAIR)
    return call(
        embed_body,
        [shape(BLOCK, WIDTH, f32), shape(BLOCK, WIDTH, bf16)],
        [own, got, tokens, final_gain],
        scalar=mine,
        after=after,
    )


def stack_body(*refs):
    for place, ref in enumerate(refs[:-1]):
        refs[-1][place * BLOCK : (place + 1) * BLOCK, :] = ref[...]


def stacked(*blocks, after=()):
    rows, columns = len(blocks) * BLOCK, blocks[0].shape[1]
    return call(stack_body, [shape(rows, columns, bf16)], list(blocks), after=after)[0]


def gather_plane(own, waited):
    before = send(own, first_ring(1))
    across = send(own, first_ring(2))
    after = send(own, first_ring(-1))
    near = (stacked(own, before, after=waited), stacked(after, across))
    left = [send(near[0], second_ring(1)), None]
    right = [None, send(near[1], second_ring(-1))]
    left[1] = send(near[1], second_ring(1))
    right[0] = send(near[0], second_ring(-1))
    far = (send(left[0], second_ring(1)), send(right[1], second_ring(-1)))
    return near, left, right, far


def passed_body(block_ref, out_ref):
    out_ref[...] = block_ref[...]


def gather_column(own, left, right, far):
    ahead = send(own, Z_OUT)
    behind = send(own, Z_BACK)
    passed = call(passed_body, [shape(BLOCK, WIDTH, bf16)], [ahead], after=[left[0], right[1]])[0]
    across = send(passed, Z_OUT)
    blocks = stacked(own, ahead, behind, across, after=[left[1], right[0], *far])
    return blocks, send(blocks, SIBLING)


def pair_chunk(images, texts, has_own):
    logits = logit_scale * contract(images, texts, 1, 1) + logit_bias
    grown = jnp.exp(logits)
    softplus = jnp.log1p(grown)
    share = grown / (1.0 + grown)
    if has_own:
        row = lax.broadcasted_iota(jnp.int32, logits.shape, 0)
        column = lax.broadcasted_iota(jnp.int32, logits.shape, 1)
        matched = (row == column) & (row < BLOCK)
        softplus = jnp.where(matched, softplus - logits, softplus)
        share = jnp.where(matched, share - 1.0, share)
    loss = jnp.sum(softplus, axis=1, keepdims=True) / total_rows
    pair_grad = (loss_scale / total_rows * share).astype(bf16)
    to_image = logit_scale * contract(pair_grad, texts, 1, 0)
    to_text = logit_scale * contract(pair_grad, images, 0, 0)
    return loss, to_image, to_text


def early_body(*refs):
    image_refs, text_refs = refs[:2], refs[2:8]
    image_ref, total_ref, loss_ref, near_ref, left_keep, left_send, right_send, right_keep = refs[8:16]
    texts = refs[16]
    for place, ref in enumerate(image_refs):
        image_ref[place * 256 : (place + 1) * 256, :] = ref[...]
    for place, ref in enumerate(text_refs):
        texts[place * 128 : (place + 1) * 128, :] = ref[...]
    loss, to_image, to_text = pair_chunk(image_ref[...], texts[...], True)
    total_ref[...] = to_image
    near_ref[...] = to_text[0:256, :]
    for place, ref in enumerate((left_keep, left_send, right_send, right_keep)):
        ref[...] = to_text[256 + place * 128 : 384 + place * 128, :].astype(ref.dtype)
    loss_ref[...] = jnp.broadcast_to(loss, (512, 128))


def late_body(image_ref, total_ref, loss_ref, far0, far1, far0_ref, far1_ref, keep_ref, send_ref, texts):
    texts[0:128, :] = far0[...]
    texts[128:256, :] = far1[...]
    loss, to_image, to_text = pair_chunk(image_ref[...], texts[...], False)
    far0_ref[...] = to_text[0:128, :].astype(bf16)
    far1_ref[...] = to_text[128:256, :].astype(bf16)
    loss = loss + loss_ref[:, 0:1]
    to_image = to_image + total_ref[...]
    pack(keep_ref, 0, to_image[0:256, :], loss[0:256, :])
    pack(send_ref, 0, to_image[256:512, :], loss[256:512, :])


def pair_tile(images, near, left, right, far):
    half32, half16 = shape(128, WIDTH, f32), shape(128, WIDTH, bf16)
    image, total, loss, near_grad, left_keep, left_send, right_send, right_keep = call(
        early_body,
        [shape(512, WIDTH, bf16), shape(512, WIDTH, f32), shape(512, 128, f32)]
        + [shape(256, WIDTH, f32), half32, half16, half16, half32],
        [*images, *near, *left, *right],
        scratch_shapes=[pltpu.VMEM((768, WIDTH), bf16)],
    )
    far0, far1, image_keep, image_send = call(
        late_body,
        [half16, half16, shape(256, PACKED, f32), shape(256, PACKED, bf16)],
        [image, total, loss, *far],
        scratch_shapes=[pltpu.VMEM((256, WIDTH), bf16)],
    )
    return near_grad, left_keep, left_send, right_send, right_keep, far0, far1, image_keep, image_send


def joined_body(keep_ref, got_ref, out_ref):
    out_ref[...] = (keep_ref[...] + got_ref[...].astype(f32)).astype(out_ref.dtype)


def near_body(near_ref, l0, l1, r0, r1, own_ref, before_ref, after_ref, across_ref):
    first = near_ref[0:128, :] + l0[...].astype(f32) + r0[...].astype(f32)
    second = near_ref[128:256, :] + l1[...].astype(f32) + r1[...].astype(f32)
    own_ref[...] = first[0:BLOCK, :]
    before_ref[...] = first[BLOCK:128, :].astype(bf16)
    after_ref[...] = second[0:BLOCK, :].astype(bf16)
    across_ref[...] = second[BLOCK:128, :].astype(bf16)


def head_back(resid, gain, d_embed):
    unit, inverse = centred(resid)
    normed = unit * gain
    scale = lax.rsqrt(jnp.sum(normed * normed, axis=-1, keepdims=True) + epsilon)
    along = jnp.sum(d_embed * normed, axis=-1, keepdims=True)
    d_normed = scale * d_embed - normed * (scale * scale * scale * along)
    return centred_back(unit, inverse, d_normed * gain)


def text_head_body(own_ref, before_ref, after_ref, across_ref, resid_ref, gain_ref, out_ref):
    d_embed = own_ref[...] + before_ref[...].astype(f32)
    d_embed = d_embed + after_ref[...].astype(f32) + across_ref[...].astype(f32)
    out_ref[...] = head_back(resid_ref[...], gain_ref[...].reshape(1, WIDTH), d_embed).astype(bf16)


def add_packed(values, loss, ref, start):
    rows = values.shape[0]
    return (
        values + ref[start : start + rows, 0:WIDTH].astype(f32),
        loss + loss_of(ref[start : start + rows, WIDTH:PACKED]),
    )


def packed_rows(ref, start, rows):
    return ref[start : start + rows, 0:WIDTH], loss_of(ref[start : start + rows, WIDTH:PACKED])


def column_first_body(keep_ref, got_ref, near_ref, across_ref):
    for place in range(3):
        values, loss = packed_rows(keep_ref, place * BLOCK, BLOCK)
        pack(near_ref, place * BLOCK, *add_packed(values, loss, got_ref, place * BLOCK))
    values, loss = packed_rows(keep_ref, 3 * BLOCK, BLOCK)
    pack(across_ref, 0, *add_packed(values, loss, got_ref, 3 * BLOCK))


def column_second_body(near_ref, got_ref, ahead_ref, behind_ref):
    values, loss = packed_rows(near_ref, BLOCK, BLOCK)
    pack(ahead_ref, 0, *add_packed(values, loss, got_ref, 0))
    pack(behind_ref, 0, *packed_rows(near_ref, 2 * BLOCK, BLOCK))


def image_head_body(near_ref, ahead_ref, behind_ref, resid_ref, gain_ref, out_ref):
    values, loss = packed_rows(near_ref, 0, BLOCK)
    values, loss = add_packed(values, loss, ahead_ref, 0)
    values, loss = add_packed(values, loss, behind_ref, 0)
    pack(out_ref, 0, head_back(resid_ref[...], gain_ref[...].reshape(1, WIDTH), values), loss)


def scatter_both(grads, keep, sent, text_head, image_head):
    near, left_keep, left_send, right_send, right_keep, far0, far1 = grads
    half16, block16 = shape(128, WIDTH, bf16), shape(BLOCK, WIDTH, bf16)
    packed16 = shape(BLOCK, PACKED, bf16)
    got = send(sent, SIBLING)
    got0 = send(far0, second_ring(-1))
    got1 = send(far1, second_ring(1))
    l1 = send(left_send, second_ring(-1))
    r0 = send(right_send, second_ring(1))
    column, across = call(column_first_body, [shape(3 * BLOCK, PACKED, f32), packed16], [keep, got])
    back = send(across, Z_BACK)

    l0 = call(joined_body, [half16], [left_keep, got0], after=[across])[0]
    r1 = call(joined_body, [half16], [right_keep, got1], after=[across])[0]
    l0 = send(l0, second_ring(-1))
    r1 = send(r1, second_ring(1))
    ahead, behind = call(column_second_body, [packed16, packed16], [column, back])
    got_ahead = send(ahead, Z_BACK)
    got_behind = send(behind, Z_OUT)

    own, before, after, across = call(
        near_body,
        [shape(BLOCK, WIDTH, f32), block16, block16, block16],
        [near, l0, l1, r0, r1],
        after=[ahead],
        flops=2 << 30,
    )
    across = send(across, first_ring(2))
    before = send(before, first_ring(-1))
    after = send(after, first_ring(1))
    image = call(image_head_body, [packed16], [column, got_ahead, got_behind, *image_head], after=[own])[0]
    text = call(text_head_body, [block16], [own, before, after, across, *text_head], after=[image], flops=2 << 30)[0]
    return image, text


def gather_rows(own):
    other = send(own, Z_PAIR)
    return own, other, send(own, SIBLING), send(other, SIBLING)


def swapped_body(own_ref, got_ref, out_ref):
    own, got = own_ref[...].astype(f32), got_ref[...].astype(f32)
    out_ref[0:BLOCK, :] = (own[0:BLOCK, :] + got[BLOCK:128, :]).astype(bf16)
    out_ref[BLOCK:128, :] = (own[BLOCK:128, :] + got[0:BLOCK, :]).astype(bf16)


def grad_body(has_loss, mine, x_ref, gain_ref, r0, r1, r2, r3, own_ref, got_ref, out_ref, *loss_ref):
    losses = jnp.zeros((1, 256), f32)
    for place in range(4):
        target = place ^ mine[0]
        start = pl.multiple_of(target * BLOCK, BLOCK)
        unit, inverse = centred(x_ref[pl.ds(start, BLOCK), :].astype(f32))
        given, norms = (r0, r1, r2, r3)[place], own_ref if place < 2 else got_ref
        rows = slice((place % 2) * BLOCK, (place % 2 + 1) * BLOCK)
        d_norm = norms[rows, :].astype(f32)
        back = centred_back(unit, inverse, d_norm * gain_ref[...].reshape(1, WIDTH))
        out_ref[pl.ds(start, BLOCK), :] = given[:, 0:WIDTH].astype(f32) + back
        if has_loss:
            row = lax.broadcasted_iota(jnp.int32, (BLOCK, 256), 0)
            column = lax.broadcasted_iota(jnp.int32, (BLOCK, 256), 1)
            loss = loss_of(given[:, WIDTH:PACKED])
            spread = jnp.where(column == target * BLOCK + row, loss, 0.0)
            losses = losses + jnp.sum(spread, axis=0, keepdims=True)
    if has_loss:
        loss_ref[0][...] = losses


def input_grad(mine, tokens, gain, blocks, keep, sent, has_loss):
    half16 = shape(128, WIDTH, bf16)
    got = send(sent, SIBLING)
    half = call(joined_body, [half16], [keep, got])[0]
    got = send(half, Z_PAIR)
    own = call(swapped_body, [half16], [half, got])[0]
    got = send(own, SIBLING)
    outs = [shape(256, WIDTH, f32)] + ([shape(1, 256, f32)] if has_loss else [])
    return call(
        functools.partial(grad_body, has_loss),
        outs,
        [tokens, gain, *blocks, own, got],
        scalar=mine,
    )


def on_device(
    image_in,
    text_in,
    image_gain,
    image_up,
    image_down,
    image_final,
    text_gain,
    text_up,
    text_down,
    text_final,
):
    mp = lax.axis_index("mp")
    mine = (2 * (mp % 2) + mp // 2).astype(jnp.int32).reshape(1)

    text_pre, keep, sent = tower_streamed(mine, text_in, text_gain, text_up, text_down)
    own, sent = scatter_half(keep, sent)
    image_pre, image_keep, image_rest = tower_forward(
        mine, image_in, image_gain, image_up, image_down, [sent]
    )
    text_resid, z_text = scattered_embed(mine, own, sent, text_in, text_final, [image_rest])
    own, sent = scatter_half(image_keep, rounded(image_rest, [z_text]))
    near, left, right, far = gather_plane(z_text, [sent])
    image_resid, z_image = scattered_embed(mine, own, sent, image_in, image_final, list(near))
    images = gather_column(z_image, left, right, far)

    *text_grads, keep, sent = pair_tile(images, near, left, right, far)
    image_own, text_own = scatter_both(
        text_grads, keep, sent, (text_resid, text_final), (image_resid, image_final)
    )
    image_dres = gather_rows(image_own)
    text_dres = gather_rows(text_own)
    keep, sent = tower_backward(image_dres, image_pre, image_up, image_down)
    text_keep, text_sent = tower_backward(text_dres, text_pre, text_up, text_down, [sent])
    image_grad, losses = input_grad(mine, image_in, image_gain, image_dres, keep, sent, True)
    text_grad = input_grad(mine, text_in, text_gain, text_dres, text_keep, text_sent, False)[0]
    return (image_grad, text_grad, losses.reshape(256))


def solution(mesh):
    placed = (
        P("dp", None),
        P("dp", None),
        P(),
        P(None, "mp"),
        P("mp", None),
        P(),
        P(),
        P(None, "mp"),
        P("mp", None),
        P(),
    )
    return jax.shard_map(
        on_device,
        mesh=mesh,
        in_specs=placed,
        out_specs=(P("dp", None), P("dp", None), P("dp")),
        check_vma=False,
    )
```
